32 devices in a mesh: slab: 8 (over z, x), plane: 4 (over y, core).
Axes of the slice: x: 2, y: 2, z: 4, core: 2. Of those that a mesh axis runs over, the one named last changes fastest.
Arguments:
- displacement: float32 [3, 64, 128, 256], P(None, 'slab', 'plane'), may hold values from -4 to 4
- velocity: float32 [3, 64, 128, 256], P(None, 'slab', 'plane'), may hold values from -4 to 4
- body_load: float32 [3, 64, 128, 256], P(None, 'slab', 'plane'), may hold values from -6 to 6
- damaged: int32 [64, 128, 256], P('slab', 'plane'), may hold values from 0 to 1, as said below
- eroded: int32 [64, 128, 256], P('slab', 'plane'), may hold values 0 or 1
- material: int32 [64, 128, 256], P('slab', 'plane'), may hold values from 0 to 7
- stiff_table: float32 [8], replicated, may hold values from 0.1 to 1
Outputs:
- new_displacement: float32 [3, 64, 128, 256], P(None, 'slab', 'plane')
- new_velocity: float32 [3, 64, 128, 256], P(None, 'slab', 'plane')
The draws below stay inside these ranges and needn't reach their ends.
Inputs may be any that keep to these rules, and one draw needn't show every extreme that they name: damaged cells cluster in one run of neighbouring blocks of 8 planes along the first dimension (a quarter of all such blocks), whose place is drawn; elsewhere they are rare.
All inputs are finite; a program needn't handle non-finite values. No bound on the sum of `eroded` on one device may be relied on, other than what follows from the above.
Results may differ from the reference program's by a relative error of at most 0.00002.
Values sent between devices are 32-bit elements; how exact they have to be, the bound alone decides.
No kernel may reach another device: no remote copies, remote signals or barrier semaphores. Data moves between devices by JAX's collectives and lax.ppermute only.
A program may use at most 64 MiB of HBM per device.

```python
import math
import jax
import jax.numpy as jnp

CX = 8
SUBSTEPS = 4
MATS = 8
NX = 64
NY = 128
NZ = 256


def draw_damaged(key, part):
    key = jax.random.fold_in(key, 5)
    slabs = NX // CX
    run_len = max(slabs // 4, 1)
    start = jax.random.randint(jax.random.fold_in(key, 11), (), 0, slabs)
    slab_of = jnp.arange(NX, dtype=jnp.int32) // CX
    inside = (slab_of - start) % slabs < run_len
    levels = jax.random.randint(jax.random.fold_in(key, 12), (NX, NY, NZ), 0, 20)
    hit = jnp.where(inside[:, None, None], levels < 18, levels < 1)
    return hit.astype(jnp.int32)


def place_ends(result, rng, least, top_value):
    extent = result.shape
    index_at = [jax.random.randint(jax.random.fold_in(rng, axis), (), 0, extent[axis]) for axis in range(len(extent))]
    result = result.at[tuple(index_at)].set(least)
    longest = extent.index(max(extent))
    index_at[longest] = (index_at[longest] + 1) % extent[longest]
    return result.at[tuple(index_at)].set(top_value)


def steps_of(rng, shape, split, low, high):
    def one(axis_at, blocks):
        heights = jax.random.uniform(jax.random.fold_in(jax.random.fold_in(rng, 6), axis_at), (blocks,), jnp.float32, low / len(split), high / len(split))
        return jnp.repeat(jnp.exp(heights), shape[axis_at] // blocks).reshape((-1,) + (1,) * (len(shape) - axis_at - 1))

    gain = one(*split[0])
    for cut in split[1:]:
        gain = gain * one(*cut)
    return gain


def noise(key, extent, deviation, reach, pieces=(), kind=jnp.bfloat16):
    result = deviation * jax.random.normal(key, extent, jnp.float32)
    if pieces:
        result = result * steps_of(key, extent, pieces, -0.22, 0.18)
    return jnp.clip(result, -reach, reach).astype(kind)


def setup_inputs(seed: int = 0) -> dict:
    arg_keys = jax.random.split(jax.random.key(seed), 8)
    displacement = noise(arg_keys[0], (3, NX, NY, NZ), 0.5, 4.0, ((1, 8), (2, 4)), jnp.float32)
    velocity = noise(arg_keys[1], (3, NX, NY, NZ), 0.5, 4.0, ((1, 8), (2, 4)), jnp.float32)
    body_load = noise(arg_keys[2], (3, NX, NY, NZ), 1.0, 6.0, ((1, 8), (2, 4)), jnp.float32)
    damaged = draw_damaged(jax.random.fold_in(arg_keys[7], 71), 0)
    eroded = place_ends((jax.random.randint(arg_keys[4], (NX, NY, NZ), 0, 8) < 1).astype(jnp.int32), jax.random.fold_in(arg_keys[4], 1), 0, 1)
    material = place_ends(jax.random.randint(arg_keys[5], (NX, NY, NZ), 0, MATS), jax.random.fold_in(arg_keys[5], 1), 0, MATS - 1).astype(jnp.int32)
    stiff_table = jnp.clip(jnp.exp(jax.random.uniform(arg_keys[6], (MATS,), jnp.float32, math.log(0.1), math.log(1.0))), 0.1, 1.0)
    return {"displacement": displacement, "velocity": velocity, "body_load": body_load, "damaged": damaged, "eroded": eroded, "material": material, "stiff_table": stiff_table}


def take(arr, dx, dy, dz):
    sx, sy, sz = arr.shape[-3], arr.shape[-2], arr.shape[-1]
    return arr[..., 1 + dx:sx - 1 + dx, 1 + dy:sy - 1 + dy, 1 + dz:sz - 1 + dz]


def forces(field, stiff):
    field_pad = jnp.pad(field, ((0, 0), (0, 0), (0, 0), (1, 1)))
    stiff_pad = jnp.pad(stiff, ((0, 0), (0, 0), (1, 1)))
    center = take(field_pad, 0, 0, 0)
    kcenter = take(stiff_pad, 0, 0, 0)
    total = jnp.zeros_like(center)
    for shift in ((1, 0, 0), (-1, 0, 0), (0, 1, 0), (0, -1, 0), (0, 0, 1), (0, 0, -1)):
        other = take(field_pad, shift[0], shift[1], shift[2])
        kface = jnp.minimum(kcenter, take(stiff_pad, shift[0], shift[1], shift[2]))
        total = total + kface[None] * (other - center)
    return total


def reference(displacement, velocity, body_load, damaged, eroded, material, stiff_table):
    stiff = stiff_table[material] * (1 - eroded).astype(jnp.float32)
    step = jnp.where(damaged == 1, 0.5 / SUBSTEPS, 0.5).astype(jnp.float32)
    stiff_ext = jnp.pad(stiff, ((1, 1), (1, 1), (0, 0)))
    for sub in range(SUBSTEPS):
        active = jnp.where((damaged == 1) | (sub == 0), 1.0, 0.0).astype(jnp.float32)
        field_ext = jnp.pad(displacement, ((0, 0), (1, 1), (1, 1), (0, 0)))
        force = forces(field_ext, stiff_ext)
        rate = (active * step)[None]
        velocity = velocity + rate * (force + body_load - 0.2 * velocity)
        displacement = displacement + rate * velocity
    return displacement, velocity
```

```python
import functools

import jax
import jax.numpy as jnp
from jax import lax
from jax.experimental import pallas as pl
from jax.experimental.pallas import tpu as pltpu
from jax.sharding import PartitionSpec as P

SUBSTEPS = 4
COARSE = 0.5
FINE = COARSE / SUBSTEPS
DRAG = 0.2
TILE = 8
AXES = ("slab", "plane")

VMEM = pl.BlockSpec(memory_space=pltpu.VMEM)
HBM = pl.BlockSpec(memory_space=pltpu.HBM)
SMALL = pltpu.CompilerParams(vmem_limit_bytes=2 << 20)


def partner(index, count, second):
    other = ((index - 1) ^ 1) + 1 if second else index ^ 1
    return other if 0 <= other < count and (index or not second) else None


def swap_pairs(slabs, planes, along_slab, second):
    pairs = []
    for s in range(slabs):
        for p in range(planes):
            if along_slab:
                other = partner(s, slabs, second)
                target = (other, p) if other is not None else (s, p ^ 1 if (p ^ 1) < planes else None)
            else:
                other = partner(p, planes, second)
                rest = planes - 1 - p if planes % 2 == 0 else None
                target = (s, other if other is not None else rest)
            if target[1] is not None and target != (s, p):
                pairs.append((s * planes + p, target[0] * planes + target[1]))
    return pairs


def has_partner(index, count, second):
    even = index % 2 == 0
    up = jnp.logical_not(even) if second else even
    return jnp.where(up, index + 1 < count, index > 0)


def pin(arrays, space):
    return [pltpu.with_memory_space_constraint(a, space) for a in arrays]


def call(kernel, shapes, arrays, aliases=None, in_hbm=(), dtypes=None, scratch=(), to_hbm=()):
    dtypes = dtypes or [jnp.float32] * len(shapes)
    out_shape = [pltpu.VMEM(s, t) for s, t in zip(shapes, dtypes)]
    out_shape += [pltpu.HBM(s, jnp.float32) for s in to_hbm]
    return pl.pallas_call(
        kernel,
        in_specs=[VMEM] * len(arrays) + [HBM] * len(in_hbm),
        out_specs=[VMEM] * len(shapes) + [HBM] * len(to_hbm),
        out_shape=out_shape,
        scratch_shapes=scratch,
        input_output_aliases=aliases or {},
        compiler_params=SMALL,
    )(*pin(arrays, pltpu.VMEM), *pin(in_hbm, pltpu.HBM))


def lookup(material, eroded, table):
    total = jnp.zeros(material.shape, jnp.float32)
    for index in range(table.shape[0]):
        total = jnp.where(material == index, table[index : index + 1, :], total)
    return total * (1 - eroded).astype(jnp.float32)


def layer(index, rows):
    return pl.ds(pl.multiple_of(index * rows, rows), rows)


def sides(cx):
    slab = lax.axis_index("slab")
    even = slab % 2 == 0
    return jnp.where(even, cx - 1, 0), jnp.where(even, 0, cx - 1)


def plane_even():
    return lax.axis_index("plane") % 2 == 0


def open_kernel(
    cx, cy, u_hbm, material_hbm, eroded_hbm, table_hbm, a, b, ya, yb, u, material, eroded, table, scalars, sems
):
    copies = [
        pltpu.make_async_copy(source, target, sems.at[i])
        for i, (source, target) in enumerate(
            ((table_hbm, scalars), (material_hbm, material), (eroded_hbm, eroded), (u_hbm, u))
        )
    ]
    for copy in copies:
        copy.start()
    copies[0].wait()
    for index in range(table.shape[0]):
        table[index : index + 1, :] = jnp.full((1, table.shape[1]), scalars[index], jnp.float32)
    for copy in copies[1:]:
        copy.wait()
    fa, fb = sides(cx)
    even = plane_even()
    for face, out in ((fa, a), (fb, b)):
        at = layer(face, cy)
        for c in range(3):
            out[c] = u[c, at, :]
        out[3] = lookup(material[at, :], eroded[at, :], table)
    for x in range(cx):
        top, end = slice(x * cy, x * cy + TILE), slice((x + 1) * cy - TILE, (x + 1) * cy)
        for c in range(4):
            if c < 3:
                first, last = u[c, top, :], u[c, end, :]
            else:
                first = lookup(material[top, :], eroded[top, :], table)
                last = lookup(material[end, :], eroded[end, :], table)
            put_rows(even, x, c, first, last, ya, yb)


def put_rows(even, x, c, first, last, ya, yb):
    first, last = first[0:1, :], last[TILE - 1 : TILE, :]
    ya[c, x : x + 1, :] = jnp.where(even, last, first)
    yb[c, x : x + 1, :] = jnp.where(even, first, last)


def advance(cx, cy, u, v, load, kx, ky, kz, rate, u_out, v_out):
    nz = u.shape[-1]

    def component(c, carry):
        here = u[c, 0:cy, :]
        below = None
        for x in range(cx):
            at = slice(x * cy, (x + 1) * cy)
            flux_y = ky[at, :] * (pltpu.roll(here, cy - 1, 0) - here)
            flux_z = kz[at, :] * (pltpu.roll(here, nz - 1, 1) - here)
            force = flux_y - pltpu.roll(flux_y, 1, 0)
            force = force + (flux_z - pltpu.roll(flux_z, 1, 1))
            if x < cx - 1:
                above = u[c, (x + 1) * cy : (x + 2) * cy, :]
                flux_x = kx[at, :] * (above - here)
                force = force + flux_x
            if x > 0:
                force = force - below
            r = rate[at, :]
            speed = v[c, at, :]
            speed = speed + r * (force + load[c, at, :] - DRAG * speed)
            v_out[c, at, :] = speed
            u_out[c, at, :] = here + r * speed
            if x < cx - 1:
                here, below = above, flux_x
        return carry

    lax.fori_loop(0, 3, component, 0)


def first_kernel(
    cx, cy, u, material, eroded, table, v_hbm, load_hbm, damaged_hbm,
    u_out, v_out, load, kx, ky, kz, coarse, fine, damaged, sems,
):
    copies = [
        pltpu.make_async_copy(source, target, sems.at[i])
        for i, (source, target) in enumerate(((damaged_hbm, damaged), (v_hbm, v_out), (load_hbm, load)))
    ]
    for copy in copies:
        copy.start()
    nz = u.shape[-1]
    row = lax.broadcasted_iota(jnp.int32, (cy, nz), 0)
    lane = lax.broadcasted_iota(jnp.int32, (cy, nz), 1)
    below = None
    for x in range(cx):
        at = slice(x * cy, (x + 1) * cy)
        k = lookup(material[at, :], eroded[at, :], table)
        ky[at, :] = jnp.where(row < cy - 1, jnp.minimum(k, pltpu.roll(k, cy - 1, 0)), 0.0)
        kz[at, :] = jnp.where(lane < nz - 1, jnp.minimum(k, pltpu.roll(k, nz - 1, 1)), 0.0)
        if x > 0:
            kx[(x - 1) * cy : x * cy, :] = jnp.minimum(below, k)
        below = k
    kx[(cx - 1) * cy : cx * cy, :] = jnp.zeros((cy, nz), jnp.float32)
    copies[0].wait()
    for x in range(cx):
        at = slice(x * cy, (x + 1) * cy)
        hit = damaged[at, :] == 1
        coarse[at, :] = jnp.where(hit, FINE, COARSE)
        fine[at, :] = jnp.where(hit, FINE, 0.0)
    for copy in copies[1:]:
        copy.wait()
    advance(cx, cy, u, v_out, load, kx, ky, kz, coarse, u_out, v_out)


def fix_face(at, u, rate, k, halo, u_new, v_new, send):
    r = rate[at, :]
    for c in range(3):
        push = r * (k * (halo[c] - u[c, at, :]))
        v_new[c, at, :] += push
        moved = u_new[c, at, :] + r * push
        u_new[c, at, :] = moved
        if send is not None:
            send[c] = moved


def fix_rows(cx, cy, u, rate, k_low, k_high, ya, yb, u_new, v_new):
    even = plane_even()
    for c in range(3):
        low = jnp.where(even, yb[c], ya[c])
        high = jnp.where(even, ya[c], yb[c])
        for x in range(cx):
            tile = slice(x * TILE, (x + 1) * TILE)
            for start, k, halo in ((x * cy, k_low, low), ((x + 1) * cy - TILE, k_high, high)):
                at = slice(start, start + TILE)
                r = rate[at, :]
                push = r * (k[tile, :] * (halo[x : x + 1, :] - u[c, at, :]))
                v_new[c, at, :] += push
                u_new[c, at, :] += r * push


def pack_rows(cx, cy, u_new, ya_send, yb_send):
    even = plane_even()
    for c in range(3):
        for x in range(cx):
            first = u_new[c, x * cy : x * cy + TILE, :]
            last = u_new[c, (x + 1) * cy - TILE : (x + 1) * cy, :]
            put_rows(even, x, c, first, last, ya_send, yb_send)


def flag(axis, second):
    return has_partner(lax.axis_index(axis), lax.axis_size(axis), second).astype(jnp.float32)


def face_stiffness(sent, received, second):
    return jnp.minimum(sent[3], received[3]) * flag("slab", second)


def row_stiffness(cx, ya_sent, yb_sent, ya, yb, k_low, k_high):
    even = plane_even()
    k_a = jnp.minimum(ya_sent[3], ya[3]) * flag("plane", False)
    k_b = jnp.minimum(yb_sent[3], yb[3]) * flag("plane", True)
    low, high = jnp.where(even, k_b, k_a), jnp.where(even, k_a, k_b)
    row = lax.broadcasted_iota(jnp.int32, (TILE, ya.shape[-1]), 0)
    for x in range(cx):
        tile = slice(x * TILE, (x + 1) * TILE)
        k_low[tile, :] = jnp.where(row == 0, low[x : x + 1, :], 0.0)
        k_high[tile, :] = jnp.where(row == TILE - 1, high[x : x + 1, :], 0.0)


def fix_a_first(
    cx, cy, u1, v1, u, rate, ha, ya, yb, a_sent, ya_sent, yb_sent, u_new, v_new, send, ka, k_low, k_high
):
    at = layer(sides(cx)[0], cy)
    row_stiffness(cx, ya_sent, yb_sent, ya, yb, k_low, k_high)
    fix_rows(cx, cy, u, rate, k_low, k_high, ya, yb, u_new, v_new)
    k = face_stiffness(a_sent, ha, False)
    ka[...] = k
    fix_face(at, u, rate, k, ha, u_new, v_new, send)


def fix_b_first(cx, cy, u1, v1, u, rate, hb, b_sent, u_new, v_new, send, ya_send, yb_send, kb):
    at = layer(sides(cx)[1], cy)
    k = face_stiffness(b_sent, hb, True)
    kb[...] = k
    fix_face(at, u, rate, k, hb, u_new, v_new, send)
    pack_rows(cx, cy, u_new, ya_send, yb_send)


def fix_a(cx, cy, u1, v1, u, rate, ha, ya, yb, ka, k_low, k_high, u_new, v_new, send):
    fix_rows(cx, cy, u, rate, k_low, k_high, ya, yb, u_new, v_new)
    fix_face(layer(sides(cx)[0], cy), u, rate, ka[...], ha, u_new, v_new, send)


def fix_b(cx, cy, u1, v1, u, rate, hb, kb, u_new, v_new, send, ya_send, yb_send):
    fix_face(layer(sides(cx)[1], cy), u, rate, kb[...], hb, u_new, v_new, send)
    pack_rows(cx, cy, u_new, ya_send, yb_send)


def last_kernel(cx, cy, u1, v1, u, rate, ha, hb, ya, yb, ka, kb, k_low, k_high, u_new, v_new, u_out, v_out, sems):
    fix_rows(cx, cy, u, rate, k_low, k_high, ya, yb, u_new, v_new)
    fa, fb = sides(cx)
    fix_face(layer(fa, cy), u, rate, ka[...], ha, u_new, v_new, None)
    fix_face(layer(fb, cy), u, rate, kb[...], hb, u_new, v_new, None)
    copies = [
        pltpu.make_async_copy(u_new, u_out, sems.at[0]),
        pltpu.make_async_copy(v_new, v_out, sems.at[1]),
    ]
    for copy in copies:
        copy.start()
    for copy in copies:
        copy.wait()


def per_device(displacement, velocity, body_load, damaged, eroded, material, stiff_table):
    _, cx, cy, nz = displacement.shape
    rows = cx * cy
    slabs, planes = lax.axis_size("slab"), lax.axis_size("plane")
    xa = swap_pairs(slabs, planes, True, False)
    xb = swap_pairs(slabs, planes, True, True)
    pa = swap_pairs(slabs, planes, False, False)
    pb = swap_pairs(slabs, planes, False, True)

    field, face, side, cells = (3, rows, nz), (3, cy, nz), (3, cx, nz), (rows, nz)
    u = displacement.reshape(field)
    v = velocity.reshape(field)
    load = body_load.reshape(field)
    damaged, eroded, material = (a.reshape(cells) for a in (damaged, eroded, material))

    def bind(kernel):
        return functools.partial(kernel, cx, cy)

    table_shape = (stiff_table.shape[0], nz)
    a, b, ya, yb, u, material, eroded, table = call(
        bind(open_kernel),
        [(4, cy, nz)] * 2 + [(4, cx, nz)] * 2 + [field, cells, cells, table_shape],
        (),
        in_hbm=(u, material, eroded, stiff_table),
        dtypes=[jnp.float32] * 5 + [jnp.int32] * 2 + [jnp.float32],
        scratch=[pltpu.SMEM(stiff_table.shape, jnp.float32), pltpu.SemaphoreType.DMA((4,))],
    )
    for sub in range(SUBSTEPS):
        ha = lax.ppermute(a, AXES, xa)
        hb = lax.ppermute(b, AXES, xb)
        hya = lax.ppermute(ya, AXES, pa)
        hyb = lax.ppermute(yb, AXES, pb)
        if sub == 0:
            u_new, v, load, kx, ky, kz, coarse, fine = call(
                bind(first_kernel),
                [field] * 3 + [cells] * 5,
                (u, material, eroded, table),
                in_hbm=(v, load, damaged),
                scratch=[pltpu.VMEM(cells, jnp.int32), pltpu.SemaphoreType.DMA((3,))],
            )
            u_new, v, a_next, ka, k_low, k_high = call(
                bind(fix_a_first),
                [field, field, face, (cy, nz), (cx * TILE, nz), (cx * TILE, nz)],
                (u_new, v, u, coarse, ha, hya, hyb, a, ya, yb),
                {0: 0, 1: 1},
            )
            u_new, v, b, ya, yb, kb = call(
                bind(fix_b_first),
                [field, field, face, side, side, (cy, nz)],
                (u_new, v, u, coarse, hb, b),
                {0: 0, 1: 1},
            )
            a = a_next
        else:
            u_new, v = call(bind(advance), [field, field], (u, v, load, kx, ky, kz, fine), {1: 1})
            if sub < SUBSTEPS - 1:
                u_new, v, a = call(
                    bind(fix_a),
                    [field, field, face],
                    (u_new, v, u, fine, ha, hya, hyb, ka, k_low, k_high),
                    {0: 0, 1: 1},
                )
                u_new, v, b, ya, yb = call(
                    bind(fix_b),
                    [field, field, face, side, side],
                    (u_new, v, u, fine, hb, kb),
                    {0: 0, 1: 1},
                )
        if sub < SUBSTEPS - 1:
            u = u_new
    out = call(
        bind(last_kernel),
        [field, field],
        (u_new, v, u, fine, ha, hb, hya, hyb, ka, kb, k_low, k_high),
        {0: 0, 1: 1},
        scratch=[pltpu.SemaphoreType.DMA((2,))],
        to_hbm=[field, field],
    )
    return out[2].reshape(displacement.shape), out[3].reshape(displacement.shape)


def solution(mesh):
    field, cells = P(None, "slab", "plane", None), P("slab", "plane", None)
    return jax.shard_map(
        per_device,
        mesh=mesh,
        in_specs=(field, field, field, cells, cells, cells, P()),
        out_specs=(field, field),
        check_vma=False,
    )
```

```python
import functools

import jax
import jax.numpy as jnp
from jax import lax
from jax.experimental import pallas as pl
from jax.experimental.pallas import tpu as pltpu
from jax.sharding import PartitionSpec as P

SUBSTEPS = 4
COARSE = 0.5
FINE = COARSE / SUBSTEPS
DRAG = 0.2
TILE = 8
LONG = 1 << 30
AXES = ("slab", "plane")

VMEM = pl.BlockSpec(memory_space=pltpu.VMEM)
HBM = pl.BlockSpec(memory_space=pltpu.HBM)
SMALL = pltpu.CompilerParams(vmem_limit_bytes=2 << 20)


def partner(index, count, second):
    other = ((index - 1) ^ 1) + 1 if second else index ^ 1
    return other if 0 <= other < count and (index or not second) else None


def swap_pairs(slabs, planes, along_slab, second):
    pairs = []
    for s in range(slabs):
        for p in range(planes):
            if along_slab:
                other = partner(s, slabs, second)
                target = (other, p) if other is not None else (s, p ^ 1 if (p ^ 1) < planes else None)
            else:
                other = partner(p, planes, second)
                rest = planes - 1 - p if planes % 2 == 0 else None
                target = (s, other if other is not None else rest)
            if target[1] is not None and target != (s, p):
                pairs.append((s * planes + p, target[0] * planes + target[1]))
    return pairs


def has_partner(index, count, second):
    even = index % 2 == 0
    up = jnp.logical_not(even) if second else even
    return jnp.where(up, index + 1 < count, index > 0)


def pin(arrays, space):
    return [pltpu.with_memory_space_constraint(a, space) for a in arrays]


def call(kernel, shapes, arrays, aliases=None, in_hbm=(), dtypes=None, scratch=(), to_hbm=(), weight=1):
    dtypes = dtypes or [jnp.float32] * len(shapes)
    out_shape = [pltpu.VMEM(s, t) for s, t in zip(shapes, dtypes)]
    out_shape += [pltpu.HBM(s, jnp.float32) for s in to_hbm]
    return pl.pallas_call(
        kernel,
        in_specs=[VMEM] * len(arrays) + [HBM] * len(in_hbm),
        out_specs=[VMEM] * len(shapes) + [HBM] * len(to_hbm),
        out_shape=out_shape,
        scratch_shapes=scratch,
        input_output_aliases=aliases or {},
        compiler_params=SMALL,
        cost_estimate=pl.CostEstimate(flops=weight, bytes_accessed=weight, transcendentals=0),
    )(*pin(arrays, pltpu.VMEM), *pin(in_hbm, pltpu.HBM))


def lookup(material, eroded, table):
    total = jnp.zeros(material.shape, jnp.float32)
    for index in range(table.shape[0]):
        total = jnp.where(material == index, table[index : index + 1, :], total)
    return total * (1 - eroded).astype(jnp.float32)


def layer(index, rows):
    return pl.ds(pl.multiple_of(index * rows, rows), rows)


def sides(cx):
    slab = lax.axis_index("slab")
    even = slab % 2 == 0
    return jnp.where(even, cx - 1, 0), jnp.where(even, 0, cx - 1)


def plane_even():
    return lax.axis_index("plane") % 2 == 0


def open_kernel(
    cx, cy, u_hbm, material_hbm, eroded_hbm, table_hbm, a, b, ya, yb, u, material, eroded, table, scalars, sems
):
    copies = [
        pltpu.make_async_copy(source, target, sems.at[i])
        for i, (source, target) in enumerate(
            ((table_hbm, scalars), (material_hbm, material), (eroded_hbm, eroded), (u_hbm, u))
        )
    ]
    for copy in copies:
        copy.start()
    copies[0].wait()
    for index in range(table.shape[0]):
        table[index : index + 1, :] = jnp.full((1, table.shape[1]), scalars[index], jnp.float32)
    for copy in copies[1:]:
        copy.wait()
    fa, fb = sides(cx)
    even = plane_even()
    for face, out in ((fa, a), (fb, b)):
        at = layer(face, cy)
        for c in range(3):
            out[c] = u[c, at, :]
        out[3] = lookup(material[at, :], eroded[at, :], table)
    for x in range(cx):
        top, end = slice(x * cy, x * cy + TILE), slice((x + 1) * cy - TILE, (x + 1) * cy)
        for c in range(4):
            if c < 3:
                first, last = u[c, top, :], u[c, end, :]
            else:
                first = lookup(material[top, :], eroded[top, :], table)
                last = lookup(material[end, :], eroded[end, :], table)
            put_rows(even, x, c, first, last, ya, yb)


def put_rows(even, x, c, first, last, ya, yb):
    first, last = first[0:1, :], last[TILE - 1 : TILE, :]
    ya[c, x : x + 1, :] = jnp.where(even, last, first)
    yb[c, x : x + 1, :] = jnp.where(even, first, last)


def advance(cx, cy, u, v, load, kx, ky, kz, rate, u_out, v_out):
    nz = u.shape[-1]

    def component(c, carry):
        here = u[c, 0:cy, :]
        below = None
        for x in range(cx):
            at = slice(x * cy, (x + 1) * cy)
            flux_y = ky[at, :] * (pltpu.roll(here, cy - 1, 0) - here)
            flux_z = kz[at, :] * (pltpu.roll(here, nz - 1, 1) - here)
            force = flux_y - pltpu.roll(flux_y, 1, 0)
            force = force + (flux_z - pltpu.roll(flux_z, 1, 1))
            if x < cx - 1:
                above = u[c, (x + 1) * cy : (x + 2) * cy, :]
                flux_x = kx[at, :] * (above - here)
                force = force + flux_x
            if x > 0:
                force = force - below
            r = rate[at, :]
            speed = v[c, at, :]
            speed = speed + r * (force + load[c, at, :] - DRAG * speed)
            v_out[c, at, :] = speed
            u_out[c, at, :] = here + r * speed
            if x < cx - 1:
                here, below = above, flux_x
        return carry

    lax.fori_loop(0, 3, component, 0)


def first_kernel(
    cx, cy, u, material, eroded, table, v_hbm, load_hbm, damaged_hbm,
    u_out, v_out, load, kx, ky, kz, coarse, fine, damaged, sems,
):
    copies = [
        pltpu.make_async_copy(source, target, sems.at[i])
        for i, (source, target) in enumerate(((damaged_hbm, damaged), (v_hbm, v_out), (load_hbm, load)))
    ]
    for copy in copies:
        copy.start()
    nz = u.shape[-1]
    row = lax.broadcasted_iota(jnp.int32, (cy, nz), 0)
    lane = lax.broadcasted_iota(jnp.int32, (cy, nz), 1)
    below = None
    for x in range(cx):
        at = slice(x * cy, (x + 1) * cy)
        k = lookup(material[at, :], eroded[at, :], table)
        ky[at, :] = jnp.where(row < cy - 1, jnp.minimum(k, pltpu.roll(k, cy - 1, 0)), 0.0)
        kz[at, :] = jnp.where(lane < nz - 1, jnp.minimum(k, pltpu.roll(k, nz - 1, 1)), 0.0)
        if x > 0:
            kx[(x - 1) * cy : x * cy, :] = jnp.minimum(below, k)
        below = k
    kx[(cx - 1) * cy : cx * cy, :] = jnp.zeros((cy, nz), jnp.float32)
    copies[0].wait()
    for x in range(cx):
        at = slice(x * cy, (x + 1) * cy)
        hit = damaged[at, :] == 1
        coarse[at, :] = jnp.where(hit, FINE, COARSE)
        fine[at, :] = jnp.where(hit, FINE, 0.0)
    for copy in copies[1:]:
        copy.wait()
    advance(cx, cy, u, v_out, load, kx, ky, kz, coarse, u_out, v_out)


def fix_face(at, u, rate, k, halo, u_new, v_new, send):
    r = rate[at, :]
    for c in range(3):
        push = r * (k * (halo[c] - u[c, at, :]))
        v_new[c, at, :] += push
        moved = u_new[c, at, :] + r * push
        u_new[c, at, :] = moved
        if send is not None:
            send[c] = moved


def fix_rows(cx, cy, u, rate, k_low, k_high, ya, yb, u_new, v_new):
    even = plane_even()
    for c in range(3):
        low = jnp.where(even, yb[c], ya[c])
        high = jnp.where(even, ya[c], yb[c])
        for x in range(cx):
            tile = slice(x * TILE, (x + 1) * TILE)
            for start, k, halo in ((x * cy, k_low, low), ((x + 1) * cy - TILE, k_high, high)):
                at = slice(start, start + TILE)
                r = rate[at, :]
                push = r * (k[tile, :] * (halo[x : x + 1, :] - u[c, at, :]))
                v_new[c, at, :] += push
                u_new[c, at, :] += r * push


def pack_rows(cx, cy, u_new, ya_send, yb_send):
    even = plane_even()
    for c in range(3):
        for x in range(cx):
            first = u_new[c, x * cy : x * cy + TILE, :]
            last = u_new[c, (x + 1) * cy - TILE : (x + 1) * cy, :]
            put_rows(even, x, c, first, last, ya_send, yb_send)


def flag(axis, second):
    return has_partner(lax.axis_index(axis), lax.axis_size(axis), second).astype(jnp.float32)


def face_stiffness(sent, received, second):
    return jnp.minimum(sent[3], received[3]) * flag("slab", second)


def row_stiffness(cx, ya_sent, yb_sent, ya, yb, k_low, k_high):
    even = plane_even()
    k_a = jnp.minimum(ya_sent[3], ya[3]) * flag("plane", False)
    k_b = jnp.minimum(yb_sent[3], yb[3]) * flag("plane", True)
    low, high = jnp.where(even, k_b, k_a), jnp.where(even, k_a, k_b)
    row = lax.broadcasted_iota(jnp.int32, (TILE, ya.shape[-1]), 0)
    for x in range(cx):
        tile = slice(x * TILE, (x + 1) * TILE)
        k_low[tile, :] = jnp.where(row == 0, low[x : x + 1, :], 0.0)
        k_high[tile, :] = jnp.where(row == TILE - 1, high[x : x + 1, :], 0.0)


def fix_b_first(
    cx, cy, u1, v1, u, rate, hb, ya, yb, b_sent, ya_sent, yb_sent, u_new, v_new, send, kb, k_low, k_high
):
    row_stiffness(cx, ya_sent, yb_sent, ya, yb, k_low, k_high)
    fix_rows(cx, cy, u, rate, k_low, k_high, ya, yb, u_new, v_new)
    k = face_stiffness(b_sent, hb, True)
    kb[...] = k
    fix_face(layer(sides(cx)[1], cy), u, rate, k, hb, u_new, v_new, send)


def fix_a_first(cx, cy, u1, v1, u, rate, ha, a_sent, u_new, v_new, send, ya_send, yb_send, ka):
    k = face_stiffness(a_sent, ha, False)
    ka[...] = k
    fix_face(layer(sides(cx)[0], cy), u, rate, k, ha, u_new, v_new, send)
    pack_rows(cx, cy, u_new, ya_send, yb_send)


def fix_b(cx, cy, u1, v1, u, rate, hb, ya, yb, kb, k_low, k_high, u_new, v_new, send):
    fix_rows(cx, cy, u, rate, k_low, k_high, ya, yb, u_new, v_new)
    fix_face(layer(sides(cx)[1], cy), u, rate, kb[...], hb, u_new, v_new, send)


def fix_a(cx, cy, u1, v1, u, rate, ha, ka, u_new, v_new, send, ya_send, yb_send):
    fix_face(layer(sides(cx)[0], cy), u, rate, ka[...], ha, u_new, v_new, send)
    pack_rows(cx, cy, u_new, ya_send, yb_send)


def hand_on(*refs):
    del refs


def after(array, other):
    return call(hand_on, [array.shape], (array, other), {0: 0})[0]


def fix_b_last(cx, cy, u1, v1, u, rate, hb, ya, yb, kb, k_low, k_high, u_new, v_new):
    fix_b(cx, cy, u1, v1, u, rate, hb, ya, yb, kb, k_low, k_high, u_new, v_new, None)


def last_kernel(cx, cy, u1, v1, u, rate, ha, ka, u_new, v_new, u_out, v_out, sems):
    fix_face(layer(sides(cx)[0], cy), u, rate, ka[...], ha, u_new, v_new, None)
    copies = [
        pltpu.make_async_copy(u_new, u_out, sems.at[0]),
        pltpu.make_async_copy(v_new, v_out, sems.at[1]),
    ]
    for copy in copies:
        copy.start()
    for copy in copies:
        copy.wait()


def per_device(displacement, velocity, body_load, damaged, eroded, material, stiff_table):
    _, cx, cy, nz = displacement.shape
    rows = cx * cy
    slabs, planes = lax.axis_size("slab"), lax.axis_size("plane")
    xa = swap_pairs(slabs, planes, True, False)
    xb = swap_pairs(slabs, planes, True, True)
    pa = swap_pairs(slabs, planes, False, False)
    pb = swap_pairs(slabs, planes, False, True)

    field, face, side, cells = (3, rows, nz), (3, cy, nz), (3, cx, nz), (rows, nz)
    u = displacement.reshape(field)
    v = velocity.reshape(field)
    load = body_load.reshape(field)
    damaged, eroded, material = (a.reshape(cells) for a in (damaged, eroded, material))

    def bind(kernel):
        return functools.partial(kernel, cx, cy)

    table_shape = (stiff_table.shape[0], nz)
    a, b, ya, yb, u, material, eroded, table = call(
        bind(open_kernel),
        [(4, cy, nz)] * 2 + [(4, cx, nz)] * 2 + [field, cells, cells, table_shape],
        (),
        in_hbm=(u, material, eroded, stiff_table),
        dtypes=[jnp.float32] * 5 + [jnp.int32] * 2 + [jnp.float32],
        scratch=[pltpu.SMEM(stiff_table.shape, jnp.float32), pltpu.SemaphoreType.DMA((4,))],
    )
    for sub in range(SUBSTEPS):
        hb = lax.ppermute(b, AXES, xb)
        if sub == 0:
            yb = after(yb, b)
        hyb = lax.ppermute(yb, AXES, pb)
        a = after(a, yb)
        ha = lax.ppermute(a, AXES, xa)
        ya = after(ya, a)
        hya = lax.ppermute(ya, AXES, pa)
        if sub == 0:
            u_new, v, load, kx, ky, kz, coarse, fine = call(
                bind(first_kernel),
                [field] * 3 + [cells] * 5,
                (u, material, eroded, table),
                in_hbm=(v, load, damaged),
                scratch=[pltpu.VMEM(cells, jnp.int32), pltpu.SemaphoreType.DMA((3,))],
            )
            u_new, v, b, kb, k_low, k_high = call(
                bind(fix_b_first),
                [field, field, face, (cy, nz), (cx * TILE, nz), (cx * TILE, nz)],
                (u_new, v, u, coarse, hb, hya, hyb, b, ya, yb),
                {0: 0, 1: 1}, weight=LONG,
            )
            u_new, v, a, ya, yb, ka = call(
                bind(fix_a_first),
                [field, field, face, side, side, (cy, nz)],
                (u_new, v, u, coarse, ha, a),
                {0: 0, 1: 1},
            )
        else:
            u_new, v = call(bind(advance), [field, field], (u, v, load, kx, ky, kz, fine), {1: 1})
            if sub < SUBSTEPS - 1:
                u_new, v, b = call(
                    bind(fix_b),
                    [field, field, face],
                    (u_new, v, u, fine, hb, hya, hyb, kb, k_low, k_high),
                    {0: 0, 1: 1}, weight=LONG,
                )
                u_new, v, a, ya, yb = call(
                    bind(fix_a),
                    [field, field, face, side, side],
                    (u_new, v, u, fine, ha, ka),
                    {0: 0, 1: 1},
                )
        if sub < SUBSTEPS - 1:
            u = u_new
    u_new, v = call(
        bind(fix_b_last), [field, field], (u_new, v, u, fine, hb, hya, hyb, kb, k_low, k_high), {0: 0, 1: 1}, weight=LONG
    )
    out = call(
        bind(last_kernel),
        [field, field],
        (u_new, v, u, fine, ha, ka),
        {0: 0, 1: 1},
        scratch=[pltpu.SemaphoreType.DMA((2,))],
        to_hbm=[field, field],
    )
    return out[2].reshape(displacement.shape), out[3].reshape(displacement.shape)


def solution(mesh):
    field, cells = P(None, "slab", "plane", None), P("slab", "plane", None)
    return jax.shard_map(
        per_device,
        mesh=mesh,
        in_specs=(field, field, field, cells, cells, cells, P()),
        out_specs=(field, field),
        check_vma=False,
    )
```

```python
import functools

import jax
import jax.numpy as jnp
from jax import lax
from jax.experimental import pallas as pl
from jax.experimental.pallas import tpu as pltpu
from jax.sharding import PartitionSpec as P

SUBSTEPS = 4
COARSE = 0.5
FINE = COARSE / SUBSTEPS
DRAG = 0.2
TILE = 8
LONG = 1 << 30
AXES = ("slab", "plane")

VMEM = pl.BlockSpec(memory_space=pltpu.VMEM)
HBM = pl.BlockSpec(memory_space=pltpu.HBM)
SMALL = pltpu.CompilerParams(vmem_limit_bytes=2 << 20)


def partner(index, count, second):
    other = ((index - 1) ^ 1) + 1 if second else index ^ 1
    return other if 0 <= other < count and (index or not second) else None


def swap_pairs(slabs, planes, along_slab, second):
    pairs = []
    for s in range(slabs):
        for p in range(planes):
            if along_slab:
                other = partner(s, slabs, second)
                target = (other, p) if other is not None else (s, p ^ 1 if (p ^ 1) < planes else None)
            else:
                other = partner(p, planes, second)
                rest = planes - 1 - p if planes % 2 == 0 else None
                target = (s, other if other is not None else rest)
            if target[1] is not None and target != (s, p):
                pairs.append((s * planes + p, target[0] * planes + target[1]))
    return pairs


def has_partner(index, count, second):
    even = index % 2 == 0
    up = jnp.logical_not(even) if second else even
    return jnp.where(up, index + 1 < count, index > 0)


def pin(arrays, space):
    return [pltpu.with_memory_space_constraint(a, space) for a in arrays]


def call(kernel, shapes, arrays, aliases=None, in_hbm=(), dtypes=None, scratch=(), to_hbm=(), weight=1):
    dtypes = dtypes or [jnp.float32] * len(shapes)
    out_shape = [pltpu.VMEM(s, t) for s, t in zip(shapes, dtypes)]
    out_shape += [pltpu.HBM(s, jnp.float32) for s in to_hbm]
    return pl.pallas_call(
        kernel,
        in_specs=[VMEM] * len(arrays) + [HBM] * len(in_hbm),
        out_specs=[VMEM] * len(shapes) + [HBM] * len(to_hbm),
        out_shape=out_shape,
        scratch_shapes=scratch,
        input_output_aliases=aliases or {},
        compiler_params=SMALL,
        cost_estimate=pl.CostEstimate(flops=weight, bytes_accessed=weight, transcendentals=0),
    )(*pin(arrays, pltpu.VMEM), *pin(in_hbm, pltpu.HBM))


def lookup(material, eroded, table):
    total = jnp.zeros(material.shape, jnp.float32)
    for index in range(table.shape[0]):
        total = jnp.where(material == index, table[index : index + 1, :], total)
    return total * (1 - eroded).astype(jnp.float32)


def layer(index, rows):
    return pl.ds(pl.multiple_of(index * rows, rows), rows)


def sides(cx):
    slab = lax.axis_index("slab")
    even = slab % 2 == 0
    return jnp.where(even, cx - 1, 0), jnp.where(even, 0, cx - 1)


def plane_even():
    return lax.axis_index("plane") % 2 == 0


def open_kernel(
    cx, cy, u_hbm, material_hbm, eroded_hbm, table_hbm, a, b, ya, yb, u, material, eroded, table, scalars, edge, sems
):
    copies = [
        pltpu.make_async_copy(source, target, sems.at[i])
        for i, (source, target) in enumerate(
            ((table_hbm, scalars), (material_hbm, material), (eroded_hbm, eroded), (u_hbm, u))
        )
    ]
    for copy in copies:
        copy.start()
    copies[0].wait()
    for index in range(table.shape[0]):
        table[index : index + 1, :] = jnp.full((1, table.shape[1]), scalars[index], jnp.float32)
    copies[1].wait()
    copies[2].wait()
    fa, fb = sides(cx)
    even = plane_even()
    for face, out in ((fa, a), (fb, b)):
        at = layer(face, cy)
        out[3] = lookup(material[at, :], eroded[at, :], table)
    for x in range(cx):
        top, end = slice(x * cy, x * cy + TILE), slice((x + 1) * cy - TILE, (x + 1) * cy)
        for i, cells in enumerate((material, eroded)):
            put_rows(even, x, i, cells[top, :], cells[end, :], edge.at[0], edge.at[1])
    for side, out in enumerate((ya, yb)):
        out[3] = lookup(edge[side, 0], edge[side, 1], table)
    copies[3].wait()
    for face, out in ((fa, a), (fb, b)):
        at = layer(face, cy)
        for c in range(3):
            out[c] = u[c, at, :]
    pack_rows(cx, cy, u, ya, yb)


def put_rows(even, x, c, first, last, ya, yb):
    first, last = first[0:1, :], last[TILE - 1 : TILE, :]
    ya[c, x : x + 1, :] = jnp.where(even, last, first)
    yb[c, x : x + 1, :] = jnp.where(even, first, last)


def advance(cx, cy, first, count, u, v, load, stiff, rate, u_out, v_out, halo=None):
    kx, ky_down, ky_up, kz_down, kz_up, total = stiff
    nz = u.shape[-1]
    row = lax.broadcasted_iota(jnp.int32, (TILE, nz), 0)
    even = plane_even()

    def tile(x, t):
        return pl.ds(pl.multiple_of(x * cy + t * TILE, TILE), TILE)

    for i in range(count):
        x = first + i
        for t in range(cy // TILE):
            at = tile(x, t)
            x_down, x_up = tile(jnp.maximum(x - 1, 0), t), tile(jnp.minimum(x + 1, cx - 1), t)
            r = rate[at, :]
            for c in range(3):
                here = u[c, at, :]
                one, two = (h[c, pl.ds(x, 1), :] for h in halo) if halo else (here, here)
                if t > 0:
                    down = pltpu.roll(u[c, tile(x, t - 1), :], 1, 0)
                else:
                    down = jnp.where(even, two, one)
                if t < cy // TILE - 1:
                    up = pltpu.roll(u[c, tile(x, t + 1), :], TILE - 1, 0)
                else:
                    up = jnp.where(even, one, two)
                down = jnp.where(row == 0, down, pltpu.roll(here, 1, 0))
                up = jnp.where(row == TILE - 1, up, pltpu.roll(here, TILE - 1, 0))
                force = (kx[at, :] * u[c, x_down, :] + kx[tile(x + 1, t), :] * u[c, x_up, :]) - total[at, :] * here
                force = force + (ky_down[at, :] * down + ky_up[at, :] * up)
                force = force + (
                    kz_down[at, :] * pltpu.roll(here, 1, 1) + kz_up[at, :] * pltpu.roll(here, nz - 1, 1)
                )
                speed = v[c, at, :]
                speed = speed + r * (force + load[c, at, :] - DRAG * speed)
                v_out[c, at, :] = speed
                u_out[c, at, :] = here + r * speed


def edge_kernel(cx, cy, u, v, load, kx, kyd, kyu, kzd, kzu, total, rate, u_out, v_out):
    advance(cx, cy, sides(cx)[1], 1, u, v, load, (kx, kyd, kyu, kzd, kzu, total), rate, u_out, v_out)


def rest_first(cx):
    return jnp.where(sides(cx)[1] == 0, 1, 0)


def rest_kernel(cx, cy, u1, v, u, load, kx, kyd, kyu, kzd, kzu, total, rate, ya, yb, u_out, v_out):
    stiff = kx, kyd, kyu, kzd, kzu, total
    advance(cx, cy, rest_first(cx), cx - 1, u, v, load, stiff, rate, u_out, v_out, (ya, yb))


def rest_kernel_first(
    cx, cy, u1, v, kyd, kyu, total, u, load, kx, kzd, kzu, rate, ya, yb, ya_sent, yb_sent,
    u_out, v_out, kyd_out, kyu_out, total_out,
):
    low, high = row_stiffness(ya_sent, yb_sent, ya, yb)
    row = lax.broadcasted_iota(jnp.int32, (TILE, u.shape[-1]), 0)
    for x in range(cx):
        for start, edge, k, out in (
            (x * cy, 0, low, kyd_out),
            ((x + 1) * cy - TILE, TILE - 1, high, kyu_out),
        ):
            at = slice(start, start + TILE)
            extra = jnp.where(row == edge, k[x : x + 1, :], 0.0)
            out[at, :] += extra
            total_out[at, :] += extra
    stiff = kx, kyd_out, kyu_out, kzd, kzu, total_out
    advance(cx, cy, rest_first(cx), cx - 1, u, v, load, stiff, rate, u_out, v_out, (ya, yb))


def prepare_kernel(
    cx, cy, u, material, eroded, table, v_hbm, load_hbm, damaged_hbm,
    u_out, v_out, load, kx, kyd, kyu, kzd, kzu, total, coarse, fine, damaged, sems,
):
    copies = [
        pltpu.make_async_copy(source, target, sems.at[i])
        for i, (source, target) in enumerate(((damaged_hbm, damaged), (v_hbm, v_out), (load_hbm, load)))
    ]
    for copy in copies:
        copy.start()
    nz = u.shape[-1]
    row = lax.broadcasted_iota(jnp.int32, (cy, nz), 0)
    lane = lax.broadcasted_iota(jnp.int32, (cy, nz), 1)
    nothing = jnp.zeros((cy, nz), jnp.float32)

    def stiffness(x):
        at = slice(x * cy, (x + 1) * cy)
        return lookup(material[at, :], eroded[at, :], table) if 0 <= x < cx else nothing

    face, k = nothing, stiffness(0)
    for x in range(cx):
        at = slice(x * cy, (x + 1) * cy)
        y_up = jnp.where(row < cy - 1, jnp.minimum(k, pltpu.roll(k, cy - 1, 0)), 0.0)
        y_down = jnp.where(row > 0, jnp.minimum(k, pltpu.roll(k, 1, 0)), 0.0)
        z_up = jnp.where(lane < nz - 1, jnp.minimum(k, pltpu.roll(k, nz - 1, 1)), 0.0)
        z_down = jnp.where(lane > 0, jnp.minimum(k, pltpu.roll(k, 1, 1)), 0.0)
        above = stiffness(x + 1)
        face_up = jnp.minimum(k, above)
        for out, value in ((kx, face), (kyu, y_up), (kyd, y_down), (kzu, z_up), (kzd, z_down)):
            out[at, :] = value
        total[at, :] = ((face + face_up) + (y_up + y_down)) + (z_up + z_down)
        face, k = face_up, above
    kx[cx * cy : (cx + 1) * cy, :] = nothing
    copies[0].wait()
    for x in range(cx):
        at = slice(x * cy, (x + 1) * cy)
        hit = damaged[at, :] == 1
        coarse[at, :] = jnp.where(hit, FINE, COARSE)
        fine[at, :] = jnp.where(hit, FINE, 0.0)
    for copy in copies[1:]:
        copy.wait()
    stiff = kx, kyd, kyu, kzd, kzu, total
    advance(cx, cy, sides(cx)[1], 1, u, v_out, load, stiff, coarse, u_out, v_out)


def fix_face(at, u, rate, k, halo, u_new, v_new, send):
    r = rate[at, :]
    for c in range(3):
        push = r * (k * (halo[c] - u[c, at, :]))
        v_new[c, at, :] += push
        moved = u_new[c, at, :] + r * push
        u_new[c, at, :] = moved
        if send is not None:
            send[c] = moved


def fix_rows(cy, x, u, rate, k_low, k_high, ya, yb, u_new, v_new):
    even = plane_even()
    for start, k, flip in ((x * cy, k_low, False), ((x + 1) * cy - TILE, k_high, True)):
        at = pl.ds(pl.multiple_of(start, TILE), TILE)
        r = rate[at, :]
        for c in range(3):
            one, two = ya[c, pl.ds(x, 1), :], yb[c, pl.ds(x, 1), :]
            halo = jnp.where(even, one, two) if flip else jnp.where(even, two, one)
            push = r * (k[...] * (halo - u[c, at, :]))
            v_new[c, at, :] += push
            u_new[c, at, :] += r * push


def pack_rows(cx, cy, u_new, ya_send, yb_send):
    even = plane_even()
    for c in range(3):
        for x in range(cx):
            first = u_new[c, x * cy : x * cy + TILE, :]
            last = u_new[c, (x + 1) * cy - TILE : (x + 1) * cy, :]
            put_rows(even, x, c, first, last, ya_send, yb_send)


def flag(axis, second):
    return has_partner(lax.axis_index(axis), lax.axis_size(axis), second).astype(jnp.float32)


def face_stiffness(sent, received, second):
    return jnp.minimum(sent[3], received[3]) * flag("slab", second)


def row_stiffness(ya_sent, yb_sent, ya, yb):
    even = plane_even()
    k_a = jnp.minimum(ya_sent[3], ya[3]) * flag("plane", False)
    k_b = jnp.minimum(yb_sent[3], yb[3]) * flag("plane", True)
    return jnp.where(even, k_b, k_a), jnp.where(even, k_a, k_b)


def fix_b_first(
    cx, cy, u1, v1, u, rate, hb, ya, yb, b_sent, ya_sent, yb_sent, u_new, v_new, send, kb, k_low, k_high, sides_k
):
    sides_k[0], sides_k[1] = row_stiffness(ya_sent, yb_sent, ya, yb)
    row = lax.broadcasted_iota(jnp.int32, k_low.shape, 0)
    face = sides(cx)[1]
    k_low[...] = jnp.where(row == 0, sides_k[0, pl.ds(face, 1), :], 0.0)
    k_high[...] = jnp.where(row == TILE - 1, sides_k[1, pl.ds(face, 1), :], 0.0)
    kb[...] = face_stiffness(b_sent, hb, True)
    fix_b(cx, cy, u1, v1, u, rate, hb, ya, yb, kb, k_low, k_high, u_new, v_new, send)


def fix_a_first(cx, cy, u1, v1, u, rate, ha, a_sent, u_new, v_new, send, ya_send, yb_send, ka):
    ka[...] = face_stiffness(a_sent, ha, False)
    fix_a(cx, cy, u1, v1, u, rate, ha, ka, u_new, v_new, send, ya_send, yb_send)


def fix_b(cx, cy, u1, v1, u, rate, hb, ya, yb, kb, k_low, k_high, u_new, v_new, send):
    face = sides(cx)[1]
    fix_rows(cy, face, u, rate, k_low, k_high, ya, yb, u_new, v_new)
    fix_face(layer(face, cy), u, rate, kb[...], hb, u_new, v_new, send)


def fix_b_last(cx, cy, u1, v1, u, rate, hb, ya, yb, kb, k_low, k_high, u_new, v_new):
    fix_b(cx, cy, u1, v1, u, rate, hb, ya, yb, kb, k_low, k_high, u_new, v_new, None)


def fix_a(cx, cy, u1, v1, u, rate, ha, ka, u_new, v_new, send, ya_send, yb_send):
    fix_face(layer(sides(cx)[0], cy), u, rate, ka[...], ha, u_new, v_new, send)
    pack_rows(cx, cy, u_new, ya_send, yb_send)


def hand_on(*refs):
    del refs


def after(array, other):
    return call(hand_on, [array.shape], (array, other), {0: 0})[0]


def last_kernel(cx, cy, u1, v1, u, rate, ha, ka, u_new, v_new, u_out, v_out, sems):
    fix_face(layer(sides(cx)[0], cy), u, rate, ka[...], ha, u_new, v_new, None)
    copies = [
        pltpu.make_async_copy(u_new, u_out, sems.at[0]),
        pltpu.make_async_copy(v_new, v_out, sems.at[1]),
    ]
    for copy in copies:
        copy.start()
    for copy in copies:
        copy.wait()


def per_device(displacement, velocity, body_load, damaged, eroded, material, stiff_table):
    _, cx, cy, nz = displacement.shape
    rows = cx * cy
    slabs, planes = lax.axis_size("slab"), lax.axis_size("plane")
    xa = swap_pairs(slabs, planes, True, False)
    xb = swap_pairs(slabs, planes, True, True)
    pa = swap_pairs(slabs, planes, False, False)
    pb = swap_pairs(slabs, planes, False, True)

    field, face, side, cells = (3, rows, nz), (3, cy, nz), (3, cx, nz), (rows, nz)
    u = displacement.reshape(field)
    v = velocity.reshape(field)
    load = body_load.reshape(field)
    damaged, eroded, material = (a.reshape(cells) for a in (damaged, eroded, material))

    def bind(kernel):
        return functools.partial(kernel, cx, cy)

    table_shape = (stiff_table.shape[0], nz)
    a, b, ya, yb, u, material, eroded, table = call(
        bind(open_kernel),
        [(4, cy, nz)] * 2 + [(4, cx, nz)] * 2 + [field, cells, cells, table_shape],
        (),
        in_hbm=(u, material, eroded, stiff_table),
        dtypes=[jnp.float32] * 5 + [jnp.int32] * 2 + [jnp.float32],
        scratch=[
            pltpu.SMEM(stiff_table.shape, jnp.float32),
            pltpu.VMEM((2, 2, cx, nz), jnp.int32),
            pltpu.SemaphoreType.DMA((4,)),
        ],
    )
    both = {0: 0, 1: 1}
    for sub in range(SUBSTEPS):
        hb = lax.ppermute(b, AXES, xb)
        if sub == 0:
            yb = after(yb, b)
        hyb = lax.ppermute(yb, AXES, pb)
        a = after(a, yb)
        ha = lax.ppermute(a, AXES, xa)
        ya = after(ya, a)
        hya = lax.ppermute(ya, AXES, pa)
        if sub == 0:
            u_new, v, load, kx, kyd, kyu, kzd, kzu, total, coarse, fine = call(
                bind(prepare_kernel),
                [field] * 3 + [((cx + 1) * cy, nz)] + [cells] * 7,
                (u, material, eroded, table),
                in_hbm=(v, load, damaged),
                scratch=[pltpu.VMEM(cells, jnp.int32), pltpu.SemaphoreType.DMA((3,))],
            )
            rate = coarse
            u_new, v, b_next, kb, k_low, k_high = call(
                bind(fix_b_first),
                [field, field, face, (cy, nz), (TILE, nz), (TILE, nz)],
                (u_new, v, u, rate, hb, hya, hyb, b, ya, yb),
                both,
                weight=LONG,
                scratch=[pltpu.VMEM((2, cx, nz), jnp.float32)],
            )
            u_new, v, kyd, kyu, total = call(
                bind(rest_kernel_first),
                [field, field] + [cells] * 3,
                (u_new, v, kyd, kyu, total, u, load, kx, kzd, kzu, rate, hya, hyb, ya, yb),
                {i: i for i in range(5)},
            )
        else:
            rate = fine
            stiff = kx, kyd, kyu, kzd, kzu, total
            u_new, v = call(bind(edge_kernel), [field, field], (u, v, load, *stiff, rate), {1: 1})
            last = sub == SUBSTEPS - 1
            u_new, v, *sent = call(
                bind(fix_b_last if last else fix_b),
                [field, field] if last else [field, field, face],
                (u_new, v, u, rate, hb, hya, hyb, kb, k_low, k_high),
                both,
                weight=LONG,
            )
            b_next = None if last else sent[0]
            u_new, v = call(
                bind(rest_kernel), [field, field], (u_new, v, u, load, *stiff, rate, hya, hyb), both
            )
        b = b_next
        if sub == 0:
            u_new, v, a, ya, yb, ka = call(
                bind(fix_a_first), [field, field, face, side, side, (cy, nz)], (u_new, v, u, rate, ha, a), both
            )
        elif sub < SUBSTEPS - 1:
            u_new, v, a, ya, yb = call(
                bind(fix_a), [field, field, face, side, side], (u_new, v, u, rate, ha, ka), both
            )
        if sub < SUBSTEPS - 1:
            u = u_new
    out = call(
        bind(last_kernel),
        [field, field],
        (u_new, v, u, fine, ha, ka),
        {0: 0, 1: 1},
        scratch=[pltpu.SemaphoreType.DMA((2,))],
        to_hbm=[field, field],
    )
    return out[2].reshape(displacement.shape), out[3].reshape(displacement.shape)


def solution(mesh):
    field, cells = P(None, "slab", "plane", None), P("slab", "plane", None)
    return jax.shard_map(
        per_device,
        mesh=mesh,
        in_specs=(field, field, field, cells, cells, cells, P()),
        out_specs=(field, field),
        check_vma=False,
    )
```

```python
import functools

import jax
import jax.numpy as jnp
from jax import lax
from jax.experimental import pallas as pl
from jax.experimental.pallas import tpu as pltpu
from jax.sharding import PartitionSpec as P

SUBSTEPS = 4
COARSE = 0.5
FINE = COARSE / SUBSTEPS
DRAG = 0.2
TILE = 8
LONG = 1 << 30
AXES = ("slab", "plane")

VMEM = pl.BlockSpec(memory_space=pltpu.VMEM)
HBM = pl.BlockSpec(memory_space=pltpu.HBM)
SMALL = pltpu.CompilerParams(vmem_limit_bytes=2 << 20)


def partner(index, count, second):
    other = ((index - 1) ^ 1) + 1 if second else index ^ 1
    return other if 0 <= other < count and (index or not second) else None


def swap_pairs(slabs, planes, along_slab, second):
    pairs = []
    for s in range(slabs):
        for p in range(planes):
            if along_slab:
                other = partner(s, slabs, second)
                target = (other, p) if other is not None else (s, p ^ 1 if (p ^ 1) < planes else None)
            else:
                other = partner(p, planes, second)
                rest = planes - 1 - p if planes % 2 == 0 else None
                target = (s, other if other is not None else rest)
            if target[1] is not None and target != (s, p):
                pairs.append((s * planes + p, target[0] * planes + target[1]))
    return pairs


def has_partner(index, count, second):
    even = index % 2 == 0
    up = jnp.logical_not(even) if second else even
    return jnp.where(up, index + 1 < count, index > 0)


def pin(arrays, space):
    return [pltpu.with_memory_space_constraint(a, space) for a in arrays]


def call(kernel, shapes, arrays, aliases=None, in_hbm=(), dtypes=None, scratch=(), to_hbm=(), weight=1):
    dtypes = dtypes or [jnp.float32] * len(shapes)
    out_shape = [pltpu.VMEM(s, t) for s, t in zip(shapes, dtypes)]
    out_shape += [pltpu.HBM(s, jnp.float32) for s in to_hbm]
    return pl.pallas_call(
        kernel,
        in_specs=[VMEM] * len(arrays) + [HBM] * len(in_hbm),
        out_specs=[VMEM] * len(shapes) + [HBM] * len(to_hbm),
        out_shape=out_shape,
        scratch_shapes=scratch,
        input_output_aliases=aliases or {},
        compiler_params=SMALL,
        cost_estimate=pl.CostEstimate(flops=weight, bytes_accessed=weight, transcendentals=0),
    )(*pin(arrays, pltpu.VMEM), *pin(in_hbm, pltpu.HBM))


def lookup(material, eroded, table):
    total = jnp.zeros(material.shape, jnp.float32)
    for index in range(table.shape[0]):
        total = jnp.where(material == index, table[index : index + 1, :], total)
    return total * (1 - eroded).astype(jnp.float32)


def layer(index, rows):
    return pl.ds(pl.multiple_of(index * rows, rows), rows)


def sides(cx):
    slab = lax.axis_index("slab")
    even = slab % 2 == 0
    return jnp.where(even, cx - 1, 0), jnp.where(even, 0, cx - 1)


def plane_even():
    return lax.axis_index("plane") % 2 == 0


def start_copies(moves, sems):
    copies = [pltpu.make_async_copy(source, target, sems.at[i]) for i, (source, target) in enumerate(moves)]
    for copy in copies:
        copy.start()
    return copies


def open_kernel(
    cx, cy, u_hbm, material_hbm, eroded_hbm, table_hbm, a, b, ya, yb, u, material, eroded, table, scalars, edge, sems
):
    moves = [(table_hbm, scalars), (material_hbm, material), (eroded_hbm, eroded)]
    copies = start_copies(moves + [(u_hbm.at[c], u.at[c]) for c in range(3)], sems)
    copies[0].wait()
    for index in range(table.shape[0]):
        table[index : index + 1, :] = jnp.full((1, table.shape[1]), scalars[index], jnp.float32)
    copies[1].wait()
    copies[2].wait()
    fa, fb = sides(cx)
    even = plane_even()
    for face, out in ((fa, a), (fb, b)):
        at = layer(face, cy)
        out[3] = lookup(material[at, :], eroded[at, :], table)
    for x in range(cx):
        top, end = slice(x * cy, x * cy + TILE), slice((x + 1) * cy - TILE, (x + 1) * cy)
        for i, cells in enumerate((material, eroded)):
            put_rows(even, x, i, cells[top, :], cells[end, :], edge.at[0], edge.at[1])
    for side, out in enumerate((ya, yb)):
        out[3] = lookup(edge[side, 0], edge[side, 1], table)
    for copy in copies[3:]:
        copy.wait()
    for face, out in ((fa, a), (fb, b)):
        at = layer(face, cy)
        for c in range(3):
            out[c] = u[c, at, :]
    pack_rows(cx, cy, u, ya, yb)


def put_rows(even, x, c, first, last, ya, yb):
    first, last = first[0:1, :], last[TILE - 1 : TILE, :]
    ya[c, x : x + 1, :] = jnp.where(even, last, first)
    yb[c, x : x + 1, :] = jnp.where(even, first, last)


def advance(cx, cy, first, count, u, v, load, stiff, rate, u_out, v_out, halo=None, then=None):
    kx, ky_down, ky_up, kz_down, kz_up, total = stiff
    nz = u.shape[-1]
    row = lax.broadcasted_iota(jnp.int32, (TILE, nz), 0)
    even = plane_even()

    def tile(x, t):
        return pl.ds(pl.multiple_of(x * cy + t * TILE, TILE), TILE)

    for i in range(count):
        x = first + i
        for t in range(cy // TILE):
            at = tile(x, t)
            x_down, x_up = tile(jnp.maximum(x - 1, 0), t), tile(jnp.minimum(x + 1, cx - 1), t)
            r = rate[at, :]
            for c in range(3):
                here = u[c, at, :]
                one, two = (h[c, pl.ds(x, 1), :] for h in halo) if halo else (here, here)
                if t > 0:
                    down = pltpu.roll(u[c, tile(x, t - 1), :], 1, 0)
                else:
                    down = jnp.where(even, two, one)
                if t < cy // TILE - 1:
                    up = pltpu.roll(u[c, tile(x, t + 1), :], TILE - 1, 0)
                else:
                    up = jnp.where(even, one, two)
                down = jnp.where(row == 0, down, pltpu.roll(here, 1, 0))
                up = jnp.where(row == TILE - 1, up, pltpu.roll(here, TILE - 1, 0))
                force = (kx[at, :] * u[c, x_down, :] + kx[tile(x + 1, t), :] * u[c, x_up, :]) - total[at, :] * here
                force = force + (ky_down[at, :] * down + ky_up[at, :] * up)
                force = force + (
                    kz_down[at, :] * pltpu.roll(here, 1, 1) + kz_up[at, :] * pltpu.roll(here, nz - 1, 1)
                )
                speed = v[c, at, :]
                speed = speed + r * (force + load[c, at, :] - DRAG * speed)
                v_out[c, at, :] = speed
                u_out[c, at, :] = here + r * speed
        if then is not None:
            then(i)


def edge_kernel(cx, cy, u, v, load, kx, kyd, kyu, kzd, kzu, total, rate, u_out, v_out):
    advance(cx, cy, sides(cx)[1], 1, u, v, load, (kx, kyd, kyu, kzd, kzu, total), rate, u_out, v_out)


def rest_first(cx):
    return jnp.where(sides(cx)[1] == 0, 1, 0)


def rest_kernel(cx, cy, u1, v, u, load, kx, kyd, kyu, kzd, kzu, total, rate, ya, yb, u_out, v_out):
    stiff = kx, kyd, kyu, kzd, kzu, total
    advance(cx, cy, rest_first(cx), cx - 1, u, v, load, stiff, rate, u_out, v_out, (ya, yb))


def rest_kernel_last(
    cx, cy, u1, v, u, load, kx, kyd, kyu, kzd, kzu, total, rate, ya, yb, u_out, v_out, u_hbm, v_hbm, sems
):
    stiff = kx, kyd, kyu, kzd, kzu, total
    start = jnp.where(sides(cx)[0] == 0, 1, 0)
    half = (cx - 1) // 2
    copies = []
    for i, (begin, size) in enumerate(((start, half), (start + half, cx - 1 - half))):
        at = pl.ds(pl.multiple_of(begin * cy, cy), size * cy)
        for j, (source, target) in enumerate(((u_out, u_hbm), (v_out, v_hbm))):
            copies.append(pltpu.make_async_copy(source.at[:, at, :], target.at[:, at, :], sems.at[2 * i + j]))

    def then(i):
        if i == half:
            copies[0].start()
            copies[1].start()

    advance(cx, cy, rest_first(cx), cx - 1, u, v, load, stiff, rate, u_out, v_out, (ya, yb), then)
    copies[2].start()
    copies[3].start()
    for copy in copies:
        copy.wait()


def rest_kernel_first(
    cx, cy, u1, v, kyd, kyu, total, u, load, kx, kzd, kzu, rate, ya, yb, ya_sent, yb_sent,
    u_out, v_out, kyd_out, kyu_out, total_out,
):
    low, high = row_stiffness(ya_sent, yb_sent, ya, yb)
    row = lax.broadcasted_iota(jnp.int32, (TILE, u.shape[-1]), 0)
    for x in range(cx):
        for start, edge, k, out in (
            (x * cy, 0, low, kyd_out),
            ((x + 1) * cy - TILE, TILE - 1, high, kyu_out),
        ):
            at = slice(start, start + TILE)
            extra = jnp.where(row == edge, k[x : x + 1, :], 0.0)
            out[at, :] += extra
            total_out[at, :] += extra
    stiff = kx, kyd_out, kyu_out, kzd, kzu, total_out
    advance(cx, cy, rest_first(cx), cx - 1, u, v, load, stiff, rate, u_out, v_out, (ya, yb))


def prepare_kernel(
    cx, cy, u, material, eroded, table, v_hbm, load_hbm, damaged_hbm,
    u_out, v_out, load, kx, kyd, kyu, kzd, kzu, total, coarse, fine, damaged, k_all, sems,
):
    moves = [(damaged_hbm, damaged)]
    moves += [(h.at[c], w.at[c]) for c in range(3) for h, w in ((v_hbm, v_out), (load_hbm, load))]
    copies = start_copies(moves, sems)
    nz = u.shape[-1]
    row = lax.broadcasted_iota(jnp.int32, (TILE, nz), 0)
    lane = lax.broadcasted_iota(jnp.int32, (TILE, nz), 1)
    nothing = jnp.zeros((TILE, nz), jnp.float32)
    tiles = cy // TILE
    for start in range(0, cx * cy, TILE):
        at = slice(start, start + TILE)
        k_all[at, :] = lookup(material[at, :], eroded[at, :], table)
    for t in range(tiles):
        face = nothing
        for x in range(cx):
            start = x * cy + t * TILE
            at = slice(start, start + TILE)
            k = k_all[at, :]
            y_up = k_all[start + TILE : start + TILE + 1, :] if t < tiles - 1 else 0.0
            y_down = k_all[start - 1 : start, :] if t > 0 else 0.0
            y_up = jnp.minimum(k, jnp.where(row == TILE - 1, y_up, pltpu.roll(k, TILE - 1, 0)))
            y_down = jnp.minimum(k, jnp.where(row == 0, y_down, pltpu.roll(k, 1, 0)))
            z_up = jnp.minimum(k, jnp.where(lane == nz - 1, 0.0, pltpu.roll(k, nz - 1, 1)))
            z_down = jnp.minimum(k, jnp.where(lane == 0, 0.0, pltpu.roll(k, 1, 1)))
            face_up = jnp.minimum(k, k_all[start + cy : start + cy + TILE, :]) if x < cx - 1 else nothing
            for out, value in ((kx, face), (kyu, y_up), (kyd, y_down), (kzu, z_up), (kzd, z_down)):
                out[at, :] = value
            total[at, :] = ((face + face_up) + (y_up + y_down)) + (z_up + z_down)
            face = face_up
    kx[cx * cy : (cx + 1) * cy, :] = jnp.zeros((cy, nz), jnp.float32)
    copies[0].wait()
    for x in range(cx):
        at = slice(x * cy, (x + 1) * cy)
        hit = damaged[at, :] == 1
        coarse[at, :] = jnp.where(hit, FINE, COARSE)
        fine[at, :] = jnp.where(hit, FINE, 0.0)
    for copy in copies[1:]:
        copy.wait()
    stiff = kx, kyd, kyu, kzd, kzu, total
    advance(cx, cy, sides(cx)[1], 1, u, v_out, load, stiff, coarse, u_out, v_out)


def fix_face(at, u, rate, k, halo, u_new, v_new, send):
    r = rate[at, :]
    for c in range(3):
        push = r * (k * (halo[c] - u[c, at, :]))
        v_new[c, at, :] += push
        moved = u_new[c, at, :] + r * push
        u_new[c, at, :] = moved
        if send is not None:
            send[c] = moved


def fix_rows(cy, x, u, rate, k_low, k_high, ya, yb, u_new, v_new):
    even = plane_even()
    for start, k, flip in ((x * cy, k_low, False), ((x + 1) * cy - TILE, k_high, True)):
        at = pl.ds(pl.multiple_of(start, TILE), TILE)
        r = rate[at, :]
        for c in range(3):
            one, two = ya[c, pl.ds(x, 1), :], yb[c, pl.ds(x, 1), :]
            halo = jnp.where(even, one, two) if flip else jnp.where(even, two, one)
            push = r * (k[...] * (halo - u[c, at, :]))
            v_new[c, at, :] += push
            u_new[c, at, :] += r * push


def pack_rows(cx, cy, u_new, ya_send, yb_send):
    even = plane_even()
    for c in range(3):
        for x in range(cx):
            first = u_new[c, x * cy : x * cy + TILE, :]
            last = u_new[c, (x + 1) * cy - TILE : (x + 1) * cy, :]
            put_rows(even, x, c, first, last, ya_send, yb_send)


def flag(axis, second):
    return has_partner(lax.axis_index(axis), lax.axis_size(axis), second).astype(jnp.float32)


def face_stiffness(sent, received, second):
    return jnp.minimum(sent[3], received[3]) * flag("slab", second)


def row_stiffness(ya_sent, yb_sent, ya, yb):
    even = plane_even()
    k_a = jnp.minimum(ya_sent[3], ya[3]) * flag("plane", False)
    k_b = jnp.minimum(yb_sent[3], yb[3]) * flag("plane", True)
    return jnp.where(even, k_b, k_a), jnp.where(even, k_a, k_b)


def fix_b_first(
    cx, cy, u1, v1, u, rate, hb, ya, yb, b_sent, ya_sent, yb_sent, u_new, v_new, send, kb, k_low, k_high, sides_k
):
    sides_k[0], sides_k[1] = row_stiffness(ya_sent, yb_sent, ya, yb)
    row = lax.broadcasted_iota(jnp.int32, k_low.shape, 0)
    face = sides(cx)[1]
    k_low[...] = jnp.where(row == 0, sides_k[0, pl.ds(face, 1), :], 0.0)
    k_high[...] = jnp.where(row == TILE - 1, sides_k[1, pl.ds(face, 1), :], 0.0)
    kb[...] = face_stiffness(b_sent, hb, True)
    fix_b(cx, cy, u1, v1, u, rate, hb, ya, yb, kb, k_low, k_high, u_new, v_new, send)


def fix_a_first(cx, cy, u1, v1, u, rate, ha, a_sent, u_new, v_new, send, ya_send, yb_send, ka):
    ka[...] = face_stiffness(a_sent, ha, False)
    fix_a(cx, cy, u1, v1, u, rate, ha, ka, u_new, v_new, send, ya_send, yb_send)


def fix_b(cx, cy, u1, v1, u, rate, hb, ya, yb, kb, k_low, k_high, u_new, v_new, send):
    face = sides(cx)[1]
    fix_rows(cy, face, u, rate, k_low, k_high, ya, yb, u_new, v_new)
    fix_face(layer(face, cy), u, rate, kb[...], hb, u_new, v_new, send)


def fix_b_last(cx, cy, u1, v1, u, rate, hb, ya, yb, kb, k_low, k_high, u_new, v_new):
    fix_b(cx, cy, u1, v1, u, rate, hb, ya, yb, kb, k_low, k_high, u_new, v_new, None)


def fix_a(cx, cy, u1, v1, u, rate, ha, ka, u_new, v_new, send, ya_send, yb_send):
    fix_face(layer(sides(cx)[0], cy), u, rate, ka[...], ha, u_new, v_new, send)
    pack_rows(cx, cy, u_new, ya_send, yb_send)


def hand_on(*refs):
    del refs


def after(array, other):
    return call(hand_on, [array.shape], (array, other), {0: 0})[0]


def last_kernel(cx, cy, u1, v1, u, rate, ha, ka, u_in, v_in, u_new, v_new, u_hbm, v_hbm, sems):
    at = layer(sides(cx)[0], cy)
    fix_face(at, u, rate, ka[...], ha, u_new, v_new, None)
    copies = [
        pltpu.make_async_copy(source.at[:, at, :], target.at[:, at, :], sems.at[i])
        for i, (source, target) in enumerate(((u_new, u_hbm), (v_new, v_hbm)))
    ]
    for copy in copies:
        copy.start()
    for copy in copies:
        copy.wait()


def per_device(displacement, velocity, body_load, damaged, eroded, material, stiff_table):
    _, cx, cy, nz = displacement.shape
    rows = cx * cy
    slabs, planes = lax.axis_size("slab"), lax.axis_size("plane")
    xa = swap_pairs(slabs, planes, True, False)
    xb = swap_pairs(slabs, planes, True, True)
    pa = swap_pairs(slabs, planes, False, False)
    pb = swap_pairs(slabs, planes, False, True)

    field, face, side, cells = (3, rows, nz), (3, cy, nz), (3, cx, nz), (rows, nz)
    u = displacement.reshape(field)
    v = velocity.reshape(field)
    load = body_load.reshape(field)
    damaged, eroded, material = (a.reshape(cells) for a in (damaged, eroded, material))

    def bind(kernel):
        return functools.partial(kernel, cx, cy)

    table_shape = (stiff_table.shape[0], nz)
    a, b, ya, yb, u, material, eroded, table = call(
        bind(open_kernel),
        [(4, cy, nz)] * 2 + [(4, cx, nz)] * 2 + [field, cells, cells, table_shape],
        (),
        in_hbm=(u, material, eroded, stiff_table),
        dtypes=[jnp.float32] * 5 + [jnp.int32] * 2 + [jnp.float32],
        scratch=[
            pltpu.SMEM(stiff_table.shape, jnp.float32),
            pltpu.VMEM((2, 2, cx, nz), jnp.int32),
            pltpu.SemaphoreType.DMA((6,)),
        ],
    )
    both = {0: 0, 1: 1}
    for sub in range(SUBSTEPS):
        hb = lax.ppermute(b, AXES, xb)
        if sub == 0:
            yb = after(yb, b)
        hyb = lax.ppermute(yb, AXES, pb)
        a = after(a, yb)
        ha = lax.ppermute(a, AXES, xa)
        ya = after(ya, a)
        hya = lax.ppermute(ya, AXES, pa)
        if sub == 0:
            u_new, v, load, kx, kyd, kyu, kzd, kzu, total, coarse, fine = call(
                bind(prepare_kernel),
                [field] * 3 + [((cx + 1) * cy, nz)] + [cells] * 7,
                (u, material, eroded, table),
                in_hbm=(v, load, damaged),
                scratch=[
                    pltpu.VMEM(cells, jnp.int32),
                    pltpu.VMEM(cells, jnp.float32),
                    pltpu.SemaphoreType.DMA((7,)),
                ],
            )
            rate = coarse
            u_new, v, b_next, kb, k_low, k_high = call(
                bind(fix_b_first),
                [field, field, face, (cy, nz), (TILE, nz), (TILE, nz)],
                (u_new, v, u, rate, hb, hya, hyb, b, ya, yb),
                both,
                weight=LONG,
                scratch=[pltpu.VMEM((2, cx, nz), jnp.float32)],
            )
            u_new, v, kyd, kyu, total = call(
                bind(rest_kernel_first),
                [field, field] + [cells] * 3,
                (u_new, v, kyd, kyu, total, u, load, kx, kzd, kzu, rate, hya, hyb, ya, yb),
                {i: i for i in range(5)},
            )
        else:
            rate = fine
            stiff = kx, kyd, kyu, kzd, kzu, total
            u_new, v = call(bind(edge_kernel), [field, field], (u, v, load, *stiff, rate), {1: 1})
            last = sub == SUBSTEPS - 1
            u_new, v, *sent = call(
                bind(fix_b_last if last else fix_b),
                [field, field] if last else [field, field, face],
                (u_new, v, u, rate, hb, hya, hyb, kb, k_low, k_high),
                both,
                weight=LONG,
            )
            b_next = None if last else sent[0]
            u_new, v, *done = call(
                bind(rest_kernel_last if last else rest_kernel),
                [field, field],
                (u_new, v, u, load, *stiff, rate, hya, hyb),
                both,
                scratch=[pltpu.SemaphoreType.DMA((4,))] if last else (),
                to_hbm=[field, field] if last else (),
            )
        b = b_next
        if sub == 0:
            u_new, v, a, ya, yb, ka = call(
                bind(fix_a_first), [field, field, face, side, side, (cy, nz)], (u_new, v, u, rate, ha, a), both
            )
        elif sub < SUBSTEPS - 1:
            u_new, v, a, ya, yb = call(
                bind(fix_a), [field, field, face, side, side], (u_new, v, u, rate, ha, ka), both
            )
        if sub < SUBSTEPS - 1:
            u = u_new
    out = call(
        bind(last_kernel),
        [field, field],
        (u_new, v, u, fine, ha, ka),
        {0: 0, 1: 1, 6: 2, 7: 3},
        in_hbm=done,
        scratch=[pltpu.SemaphoreType.DMA((2,))],
        to_hbm=[field, field],
    )
    return out[2].reshape(displacement.shape), out[3].reshape(displacement.shape)


def solution(mesh):
    field, cells = P(None, "slab", "plane", None), P("slab", "plane", None)
    return jax.shard_map(
        per_device,
        mesh=mesh,
        in_specs=(field, field, field, cells, cells, cells, P()),
        out_specs=(field, field),
        check_vma=False,
    )
```

```python
import functools

import jax
import jax.numpy as jnp
from jax import lax
from jax.experimental import pallas as pl
from jax.experimental.pallas import tpu as pltpu
from jax.sharding import PartitionSpec as P

SUBSTEPS = 4
COARSE = 0.5
FINE = COARSE / SUBSTEPS
DRAG = 0.2
TILE = 8
LONG = 1 << 30
AXES = ("slab", "plane")

VMEM = pl.BlockSpec(memory_space=pltpu.VMEM)
HBM = pl.BlockSpec(memory_space=pltpu.HBM)
SMALL = pltpu.CompilerParams(vmem_limit_bytes=2 << 20)


def partner(index, count, second):
    other = ((index - 1) ^ 1) + 1 if second else index ^ 1
    return other if 0 <= other < count and (index or not second) else None


def swap_pairs(slabs, planes, along_slab, second):
    pairs = []
    for s in range(slabs):
        for p in range(planes):
            if along_slab:
                other = partner(s, slabs, second)
                target = (other, p) if other is not None else (s, p ^ 1 if (p ^ 1) < planes else None)
            else:
                other = partner(p, planes, second)
                rest = planes - 1 - p if planes % 2 == 0 else None
                target = (s, other if other is not None else rest)
            if target[1] is not None and target != (s, p):
                pairs.append((s * planes + p, target[0] * planes + target[1]))
    return pairs


def has_partner(index, count, second):
    even = index % 2 == 0
    up = jnp.logical_not(even) if second else even
    return jnp.where(up, index + 1 < count, index > 0)


def pin(arrays, space):
    return [pltpu.with_memory_space_constraint(a, space) for a in arrays]


def call(kernel, shapes, arrays, aliases=None, in_hbm=(), dtypes=None, scratch=(), to_hbm=(), weight=1):
    dtypes = dtypes or [jnp.float32] * len(shapes)
    out_shape = [pltpu.VMEM(s, t) for s, t in zip(shapes, dtypes)]
    out_shape += [pltpu.HBM(s, jnp.float32) for s in to_hbm]
    return pl.pallas_call(
        kernel,
        in_specs=[VMEM] * len(arrays) + [HBM] * len(in_hbm),
        out_specs=[VMEM] * len(shapes) + [HBM] * len(to_hbm),
        out_shape=out_shape,
        scratch_shapes=scratch,
        input_output_aliases=aliases or {},
        compiler_params=SMALL,
        cost_estimate=pl.CostEstimate(flops=weight, bytes_accessed=weight, transcendentals=0),
    )(*pin(arrays, pltpu.VMEM), *pin(in_hbm, pltpu.HBM))


def lookup(material, eroded, table):
    total = jnp.zeros(material.shape, jnp.float32)
    for index in range(table.shape[0]):
        total = jnp.where(material == index, table[index : index + 1, :], total)
    return total * (1 - eroded).astype(jnp.float32)


def layer(index, rows):
    return pl.ds(pl.multiple_of(index * rows, rows), rows)


def sides(cx):
    slab = lax.axis_index("slab")
    even = slab % 2 == 0
    return jnp.where(even, cx - 1, 0), jnp.where(even, 0, cx - 1)


def plane_even():
    return lax.axis_index("plane") % 2 == 0


def start_copies(moves, sems):
    copies = [pltpu.make_async_copy(source, target, sems.at[i]) for i, (source, target) in enumerate(moves)]
    for copy in copies:
        copy.start()
    return copies


def open_kernel(
    cx, cy, u_hbm, material_hbm, eroded_hbm, table_hbm, a, b, ya, yb, u, material, eroded, table, scalars, edge, sems
):
    moves = [(table_hbm, scalars), (material_hbm, material), (eroded_hbm, eroded)]
    copies = start_copies(moves + [(u_hbm.at[c], u.at[c]) for c in range(3)], sems)
    copies[0].wait()
    for index in range(table.shape[0]):
        table[index : index + 1, :] = jnp.full((1, table.shape[1]), scalars[index], jnp.float32)
    copies[1].wait()
    copies[2].wait()
    fa, fb = sides(cx)
    even = plane_even()
    for face, out in ((fa, a), (fb, b)):
        at = layer(face, cy)
        out[3] = lookup(material[at, :], eroded[at, :], table)
    for x in range(cx):
        top, end = slice(x * cy, x * cy + TILE), slice((x + 1) * cy - TILE, (x + 1) * cy)
        for i, cells in enumerate((material, eroded)):
            put_rows(even, x, i, cells[top, :], cells[end, :], edge.at[0], edge.at[1])
    for side, out in enumerate((ya, yb)):
        out[3] = lookup(edge[side, 0], edge[side, 1], table)
    for copy in copies[3:]:
        copy.wait()
    for face, out in ((fa, a), (fb, b)):
        at = layer(face, cy)
        for c in range(3):
            out[c] = u[c, at, :]
    pack_rows(cx, cy, u, ya, yb)


def put_rows(even, x, c, first, last, ya, yb):
    first, last = first[0:1, :], last[TILE - 1 : TILE, :]
    ya[c, x : x + 1, :] = jnp.where(even, last, first)
    yb[c, x : x + 1, :] = jnp.where(even, first, last)


def advance(cx, cy, first, count, u, v, load, stiff, rate, u_out, v_out, halo=None, then=None, tiles=None):
    kx, ky_down, ky_up, kz_down, kz_up, total = stiff
    nz = u.shape[-1]
    row = lax.broadcasted_iota(jnp.int32, (TILE, nz), 0)
    even = plane_even()

    def tile(x, t):
        return pl.ds(pl.multiple_of(x * cy + t * TILE, TILE), TILE)

    for i in range(count):
        x = first + i
        for t in tiles if tiles is not None else range(cy // TILE):
            at = tile(x, t)
            x_down, x_up = tile(jnp.maximum(x - 1, 0), t), tile(jnp.minimum(x + 1, cx - 1), t)
            r = rate[at, :]
            for c in range(3):
                here = u[c, at, :]
                one, two = (h[c, pl.ds(x, 1), :] for h in halo) if halo else (here, here)
                if t > 0:
                    down = pltpu.roll(u[c, tile(x, t - 1), :], 1, 0)
                else:
                    down = jnp.where(even, two, one)
                if t < cy // TILE - 1:
                    up = pltpu.roll(u[c, tile(x, t + 1), :], TILE - 1, 0)
                else:
                    up = jnp.where(even, one, two)
                down = jnp.where(row == 0, down, pltpu.roll(here, 1, 0))
                up = jnp.where(row == TILE - 1, up, pltpu.roll(here, TILE - 1, 0))
                force = (kx[at, :] * u[c, x_down, :] + kx[tile(x + 1, t), :] * u[c, x_up, :]) - total[at, :] * here
                force = force + (ky_down[at, :] * down + ky_up[at, :] * up)
                force = force + (
                    kz_down[at, :] * pltpu.roll(here, 1, 1) + kz_up[at, :] * pltpu.roll(here, nz - 1, 1)
                )
                speed = v[c, at, :]
                speed = speed + r * (force + load[c, at, :] - DRAG * speed)
                v_out[c, at, :] = speed
                u_out[c, at, :] = here + r * speed
        if then is not None:
            then(i)


def rest_first(cx):
    return jnp.where(sides(cx)[1] == 0, 1, 0)


def advance_inner(cx, cy, u, v, load, stiff, rate, u_out, v_out):
    advance(cx, cy, sides(cx)[1], 1, u, v, load, stiff, rate, u_out, v_out)
    inner = range(1, cy // TILE - 1)
    advance(cx, cy, rest_first(cx), cx - 1, u, v, load, stiff, rate, u_out, v_out, tiles=inner)


def advance_outer(cx, cy, u, v, load, stiff, rate, u_out, v_out, halo, then=None):
    outer = sorted({0, cy // TILE - 1})
    advance(cx, cy, rest_first(cx), cx - 1, u, v, load, stiff, rate, u_out, v_out, halo, then, outer)


def edge_kernel(cx, cy, u, v, load, kx, kyd, kyu, kzd, kzu, total, rate, u_out, v_out):
    advance_inner(cx, cy, u, v, load, (kx, kyd, kyu, kzd, kzu, total), rate, u_out, v_out)


def rest_kernel(
    cx, cy, u1, v, u, load, kx, kyd, kyu, kzd, kzu, total, rate, ya, yb, u_out, v_out, ya_send, yb_send
):
    stiff = kx, kyd, kyu, kzd, kzu, total
    advance_outer(cx, cy, u, v, load, stiff, rate, u_out, v_out, (ya, yb))
    pack_rows(cx, cy, u_out, ya_send, yb_send)


def rest_kernel_last(
    cx, cy, u1, v, u, load, kx, kyd, kyu, kzd, kzu, total, rate, ya, yb, u_out, v_out, u_hbm, v_hbm, sems
):
    stiff = kx, kyd, kyu, kzd, kzu, total
    start = jnp.where(sides(cx)[0] == 0, 1, 0)
    half = (cx - 1) // 2
    copies = []
    for i, (begin, size) in enumerate(((start, half), (start + half, cx - 1 - half))):
        at = pl.ds(pl.multiple_of(begin * cy, cy), size * cy)
        for j, (source, target) in enumerate(((u_out, u_hbm), (v_out, v_hbm))):
            copies.append(pltpu.make_async_copy(source.at[:, at, :], target.at[:, at, :], sems.at[2 * i + j]))

    def then(i):
        if i == half:
            copies[0].start()
            copies[1].start()

    advance_outer(cx, cy, u, v, load, stiff, rate, u_out, v_out, (ya, yb), then)
    copies[2].start()
    copies[3].start()
    for copy in copies:
        copy.wait()


def rest_kernel_first(
    cx, cy, u1, v, kyd, kyu, total, u, load, kx, kzd, kzu, rate, fine, ya, yb, ya_sent, yb_sent,
    u_out, v_out, kyd_out, kyu_out, total_out, ya_send, yb_send,
):
    low, high = row_stiffness(ya_sent, yb_sent, ya, yb)
    row = lax.broadcasted_iota(jnp.int32, (TILE, u.shape[-1]), 0)
    for x in range(cx):
        for start, edge, k, out in (
            (x * cy, 0, low, kyd_out),
            ((x + 1) * cy - TILE, TILE - 1, high, kyu_out),
        ):
            at = slice(start, start + TILE)
            extra = jnp.where(row == edge, k[x : x + 1, :], 0.0)
            out[at, :] += extra
            total_out[at, :] += extra
    stiff = kx, kyd_out, kyu_out, kzd, kzu, total_out
    advance_outer(cx, cy, u, v, load, stiff, rate, u_out, v_out, (ya, yb))
    pack_rows(cx, cy, u_out, ya_send, yb_send, fine)


def prepare_kernel(
    cx, cy, u, material, eroded, table, v_hbm, load_hbm, damaged_hbm,
    u_out, v_out, load, kx, kyd, kyu, kzd, kzu, total, coarse, fine, damaged, k_all, sems,
):
    moves = [(damaged_hbm, damaged)]
    moves += [(h.at[c], w.at[c]) for c in range(3) for h, w in ((v_hbm, v_out), (load_hbm, load))]
    copies = start_copies(moves, sems)
    nz = u.shape[-1]
    row = lax.broadcasted_iota(jnp.int32, (TILE, nz), 0)
    lane = lax.broadcasted_iota(jnp.int32, (TILE, nz), 1)
    nothing = jnp.zeros((TILE, nz), jnp.float32)
    tiles = cy // TILE
    for start in range(0, cx * cy, TILE):
        at = slice(start, start + TILE)
        k_all[at, :] = lookup(material[at, :], eroded[at, :], table)
    for t in range(tiles):
        face = nothing
        for x in range(cx):
            start = x * cy + t * TILE
            at = slice(start, start + TILE)
            k = k_all[at, :]
            y_up = k_all[start + TILE : start + TILE + 1, :] if t < tiles - 1 else 0.0
            y_down = k_all[start - 1 : start, :] if t > 0 else 0.0
            y_up = jnp.minimum(k, jnp.where(row == TILE - 1, y_up, pltpu.roll(k, TILE - 1, 0)))
            y_down = jnp.minimum(k, jnp.where(row == 0, y_down, pltpu.roll(k, 1, 0)))
            z_up = jnp.minimum(k, jnp.where(lane == nz - 1, 0.0, pltpu.roll(k, nz - 1, 1)))
            z_down = jnp.minimum(k, jnp.where(lane == 0, 0.0, pltpu.roll(k, 1, 1)))
            face_up = jnp.minimum(k, k_all[start + cy : start + cy + TILE, :]) if x < cx - 1 else nothing
            for out, value in ((kx, face), (kyu, y_up), (kyd, y_down), (kzu, z_up), (kzd, z_down)):
                out[at, :] = value
            total[at, :] = ((face + face_up) + (y_up + y_down)) + (z_up + z_down)
            face = face_up
    kx[cx * cy : (cx + 1) * cy, :] = jnp.zeros((cy, nz), jnp.float32)
    copies[0].wait()
    for x in range(cx):
        at = slice(x * cy, (x + 1) * cy)
        hit = damaged[at, :] == 1
        coarse[at, :] = jnp.where(hit, FINE, COARSE)
        fine[at, :] = jnp.where(hit, FINE, 0.0)
    for copy in copies[1:]:
        copy.wait()
    stiff = kx, kyd, kyu, kzd, kzu, total
    advance_inner(cx, cy, u, v_out, load, stiff, coarse, u_out, v_out)


def fix_face(at, u, rate, k, halo, u_new, v_new, put=None):
    r = rate[at, :]
    for c in range(3):
        push = r * (k * (halo(c) - u[c, at, :]))
        v_new[c, at, :] += push
        moved = u_new[c, at, :] + r * push
        u_new[c, at, :] = moved
        if put is not None:
            put(c, moved)


def fix_rows(cy, x, u, rate, k_low, k_high, ya, yb, u_new, v_new):
    even = plane_even()
    for start, k, flip in ((x * cy, k_low, False), ((x + 1) * cy - TILE, k_high, True)):
        at = pl.ds(pl.multiple_of(start, TILE), TILE)
        r = rate[at, :]
        for c in range(3):
            one, two = ya[c, pl.ds(x, 1), :], yb[c, pl.ds(x, 1), :]
            halo = jnp.where(even, one, two) if flip else jnp.where(even, two, one)
            push = r * (k[...] * (halo - u[c, at, :]))
            v_new[c, at, :] += push
            u_new[c, at, :] += r * push


def pack_rows(cx, cy, u_new, ya_send, yb_send, cells=None):
    even = plane_even()
    for c in range(3 if cells is None else 4):
        for x in range(cx):
            top, end = slice(x * cy, x * cy + TILE), slice((x + 1) * cy - TILE, (x + 1) * cy)
            if c < 3:
                first, last = u_new[c, top, :], u_new[c, end, :]
            else:
                first, last = cells[top, :], cells[end, :]
            put_rows(even, x, c, first, last, ya_send, yb_send)


def flag(axis, second):
    return has_partner(lax.axis_index(axis), lax.axis_size(axis), second).astype(jnp.float32)


def face_stiffness(sent, received, second):
    return jnp.minimum(sent[3], received[3]) * flag("slab", second)


def row_stiffness(ya_sent, yb_sent, ya, yb):
    even = plane_even()
    k_a = jnp.minimum(ya_sent[3], ya[3]) * flag("plane", False)
    k_b = jnp.minimum(yb_sent[3], yb[3]) * flag("plane", True)
    return jnp.where(even, k_b, k_a), jnp.where(even, k_a, k_b)


def fix_b_first(
    cx, cy, u1, v1, u, rate, hb, ya, yb, b_sent, ya_sent, yb_sent, u_new, v_new, send, kb, k_low, k_high, sides_k
):
    sides_k[0], sides_k[1] = row_stiffness(ya_sent, yb_sent, ya, yb)
    row = lax.broadcasted_iota(jnp.int32, k_low.shape, 0)
    face = sides(cx)[1]
    k_low[...] = jnp.where(row == 0, sides_k[0, pl.ds(face, 1), :], 0.0)
    k_high[...] = jnp.where(row == TILE - 1, sides_k[1, pl.ds(face, 1), :], 0.0)
    kb[...] = face_stiffness(b_sent, hb, True)
    fix_b(cx, cy, u1, v1, u, rate, hb, ya, yb, kb, k_low, k_high, u_new, v_new, send)


def fix_b(cx, cy, u1, v1, u, rate, hb, ya, yb, kb, k_low, k_high, u_new, v_new, send=None):
    face = sides(cx)[1]
    fix_rows(cy, face, u, rate, k_low, k_high, ya, yb, u_new, v_new)

    def put(c, moved):
        if send is not None:
            send[c] = moved

    fix_face(layer(face, cy), u, rate, kb[...], lambda c: hb[c], u_new, v_new, put)


def put_face(cy, send):
    def put(c, moved):
        send[c * cy : (c + 1) * cy, :] = moved

    return put


def put_halos(cy, x, ya, yb, send):
    for c in range(4):
        if c < ya.shape[0]:
            rows = halo_rows(ya, yb, c, x)
        else:
            rows = [jnp.zeros((1, send.shape[1]), jnp.float32)] * 2
        for side in range(2):
            at = 3 * cy + 4 * side + c
            send[at : at + 1, :] = rows[side]


def halo_rows(ya, yb, c, x):
    even = plane_even()
    one, two = ya[c, pl.ds(x, 1), :], yb[c, pl.ds(x, 1), :]
    return jnp.where(even, two, one), jnp.where(even, one, two)


def coarse_of(fine):
    return COARSE + (FINE - COARSE) / FINE * fine


def correct(cx, cy, step, rate, ha, ya, yb, kyd, kyu, old_ya, old_yb, state, u_new, v_new, state_out):
    face = sides(cx)[0]
    row = lax.broadcasted_iota(jnp.int32, (TILE, rate.shape[1]), 0)
    for side in range(2):
        def sent(f, base=3 * cy + 4 * side):
            return ha[base + f : base + f + 1, :]

        def kept(f, side=side):
            return state[side, f : f + 1, :]

        if step == 1:
            k = jnp.minimum(halo_rows(old_ya, old_yb, 3, face)[side], sent(3)) * flag("slab", False)
            mine = halo_rows(ya, yb, 3, face)[side]
            other = jnp.zeros_like(mine)
            scale = coarse_of(mine) * coarse_of(mine) * k
        else:
            k, mine = kept(9), kept(10)
            other = sent(3) if step == 2 else kept(11)
            scale = mine * mine * k
            pace = coarse_of(other) if step == 2 else other
            pace = pace * pace * k
        start = face * cy if side == 0 else (face + 1) * cy - TILE
        at = pl.ds(pl.multiple_of(start, TILE), TILE)
        edge_k = jnp.where(row == (0 if side == 0 else TILE - 1), (kyd if side == 0 else kyu)[at, :], 0.0)
        r = rate[at, :]
        for c in range(3):
            if step == 1:
                before, across = halo_rows(old_ya, old_yb, c, face)[side], sent(c)
            else:
                before = kept(c)
                across = sent(c) + pace * (kept(3 + c) - kept(6 + c))
            late = scale * (across - before)
            push = r * (edge_k * late)
            v_new[c, at, :] += push
            u_new[c, at, :] += r * push
            if state_out is not None:
                now = halo_rows(ya, yb, c, face)[side] + late
                for f, value in ((c, now), (3 + c, before), (6 + c, across)):
                    state_out[side, f : f + 1, :] = value
        if state_out is not None:
            for f, value in ((9, k), (10, mine), (11, other)):
                state_out[side, f : f + 1, :] = value


def fix_a_first(cx, cy, u1, v1, u, rate, ha, a_sent, ya, yb, u_new, v_new, send, ka):
    ka[...] = face_stiffness(a_sent, ha, False)
    face = sides(cx)[0]
    put_halos(cy, face, ya, yb, send)
    fix_face(layer(face, cy), u, rate, ka[...], lambda c: ha[c], u_new, v_new, put_face(cy, send))


def fix_a_second(
    cx, cy, u1, v1, u, rate, ha, ka, ya, yb, kyd, kyu, old_ya, old_yb, u_new, v_new, send, state_out
):
    correct(cx, cy, 1, rate, ha, ya, yb, kyd, kyu, old_ya, old_yb, None, u_new, v_new, state_out)
    finish_a(cx, cy, u, rate, ha, ka, ya, yb, u_new, v_new, send)


def fix_a_third(cx, cy, u1, v1, u, rate, ha, ka, ya, yb, kyd, kyu, state, u_new, v_new, send, state_out):
    correct(cx, cy, 2, rate, ha, ya, yb, kyd, kyu, None, None, state, u_new, v_new, state_out)
    finish_a(cx, cy, u, rate, ha, ka, ya, yb, u_new, v_new, send)


def finish_a(cx, cy, u, rate, ha, ka, ya, yb, u_new, v_new, send):
    face = sides(cx)[0]
    put_halos(cy, face, ya, yb, send)
    fix_face(
        layer(face, cy), u, rate, ka[...], lambda c: ha[c * cy : (c + 1) * cy, :], u_new, v_new, put_face(cy, send)
    )


def hand_on(*refs):
    del refs


def after(array, other):
    return call(hand_on, [array.shape], (array, other), {0: 0})[0]


def last_kernel(
    cx, cy, u1, v1, u, rate, ha, ka, ya, yb, kyd, kyu, state, u_in, v_in, u_new, v_new, u_hbm, v_hbm, sems
):
    at = layer(sides(cx)[0], cy)
    correct(cx, cy, 3, rate, ha, ya, yb, kyd, kyu, None, None, state, u_new, v_new, None)
    fix_face(at, u, rate, ka[...], lambda c: ha[c * cy : (c + 1) * cy, :], u_new, v_new)
    copies = [
        pltpu.make_async_copy(source.at[:, at, :], target.at[:, at, :], sems.at[i])
        for i, (source, target) in enumerate(((u_new, u_hbm), (v_new, v_hbm)))
    ]
    for copy in copies:
        copy.start()
    for copy in copies:
        copy.wait()


def per_device(displacement, velocity, body_load, damaged, eroded, material, stiff_table):
    _, cx, cy, nz = displacement.shape
    rows = cx * cy
    slabs, planes = lax.axis_size("slab"), lax.axis_size("plane")
    xa = swap_pairs(slabs, planes, True, False)
    xb = swap_pairs(slabs, planes, True, True)
    pa = swap_pairs(slabs, planes, False, False)
    pb = swap_pairs(slabs, planes, False, True)

    field, face, side, cells = (3, rows, nz), (3, cy, nz), (3, cx, nz), (rows, nz)
    u = displacement.reshape(field)
    v = velocity.reshape(field)
    load = body_load.reshape(field)
    damaged, eroded, material = (a.reshape(cells) for a in (damaged, eroded, material))

    def bind(kernel):
        return functools.partial(kernel, cx, cy)

    table_shape = (stiff_table.shape[0], nz)
    a, b, ya, yb, u, material, eroded, table = call(
        bind(open_kernel),
        [(4, cy, nz)] * 2 + [(4, cx, nz)] * 2 + [field, cells, cells, table_shape],
        (),
        in_hbm=(u, material, eroded, stiff_table),
        dtypes=[jnp.float32] * 5 + [jnp.int32] * 2 + [jnp.float32],
        scratch=[
            pltpu.SMEM(stiff_table.shape, jnp.float32),
            pltpu.VMEM((2, 2, cx, nz), jnp.int32),
            pltpu.SemaphoreType.DMA((6,)),
        ],
    )
    both = {0: 0, 1: 1}
    for sub in range(SUBSTEPS):
        hb = lax.ppermute(b, AXES, xb)
        if sub == 0:
            yb = after(yb, b)
        hyb = lax.ppermute(yb, AXES, pb)
        if sub == 0:
            a = after(a, yb)
        ha = lax.ppermute(a, AXES, xa)
        hya = lax.ppermute(ya, AXES, pa)
        if sub == 0:
            u_new, v, load, kx, kyd, kyu, kzd, kzu, total, coarse, fine = call(
                bind(prepare_kernel),
                [field] * 3 + [((cx + 1) * cy, nz)] + [cells] * 7,
                (u, material, eroded, table),
                in_hbm=(v, load, damaged),
                scratch=[
                    pltpu.VMEM(cells, jnp.int32),
                    pltpu.VMEM(cells, jnp.float32),
                    pltpu.SemaphoreType.DMA((7,)),
                ],
            )
            rate = coarse
            u_new, v, b_next, kb, k_low, k_high = call(
                bind(fix_b_first),
                [field, field, face, (cy, nz), (TILE, nz), (TILE, nz)],
                (u_new, v, u, rate, hb, hya, hyb, b, ya, yb),
                both,
                weight=LONG,
                scratch=[pltpu.VMEM((2, cx, nz), jnp.float32)],
            )
            u_new, v, kyd, kyu, total, *sides_next = call(
                bind(rest_kernel_first),
                [field, field] + [cells] * 3 + [(4, cx, nz)] * 2,
                (u_new, v, kyd, kyu, total, u, load, kx, kzd, kzu, rate, fine, hya, hyb, ya, yb),
                {i: i for i in range(5)},
            )
        else:
            rate = fine
            stiff = kx, kyd, kyu, kzd, kzu, total
            u_new, v = call(bind(edge_kernel), [field, field], (u, v, load, *stiff, rate), {1: 1})
            last = sub == SUBSTEPS - 1
            u_new, v, *sent = call(
                bind(fix_b),
                [field, field] if last else [field, field, face],
                (u_new, v, u, rate, hb, hya, hyb, kb, k_low, k_high),
                both,
                weight=LONG,
            )
            b_next = None if last else sent[0]
            u_new, v, *rest = call(
                bind(rest_kernel_last if last else rest_kernel),
                [field, field] if last else [field, field, side, side],
                (u_new, v, u, load, *stiff, rate, hya, hyb),
                both,
                scratch=[pltpu.SemaphoreType.DMA((4,))] if last else (),
                to_hbm=[field, field] if last else (),
            )
            sides_next = None if last else rest
        b = b_next
        face_and_halos, state_shape = (3 * cy + TILE, nz), (2, 16, nz)
        if sub == 0:
            u_new, v, a, ka = call(
                bind(fix_a_first),
                [field, field, face_and_halos, (cy, nz)],
                (u_new, v, u, rate, ha, a, hya, hyb),
                both,
            )
            old = hya, hyb
        elif sub < SUBSTEPS - 1:
            u_new, v, a, *old = call(
                bind(fix_a_second if sub == 1 else fix_a_third),
                [field, field, face_and_halos, state_shape],
                (u_new, v, u, rate, ha, ka, hya, hyb, kyd, kyu, *old),
                both,
            )
        if sub < SUBSTEPS - 1:
            u = u_new
            ya, yb = sides_next
    out = call(
        bind(last_kernel),
        [field, field],
        (u_new, v, u, fine, ha, ka, hya, hyb, kyd, kyu, *old),
        {0: 0, 1: 1, 11: 2, 12: 3},
        in_hbm=rest,
        scratch=[pltpu.SemaphoreType.DMA((2,))],
        to_hbm=[field, field],
    )
    return out[2].reshape(displacement.shape), out[3].reshape(displacement.shape)


def solution(mesh):
    field, cells = P(None, "slab", "plane", None), P("slab", "plane", None)
    return jax.shard_map(
        per_device,
        mesh=mesh,
        in_specs=(field, field, field, cells, cells, cells, P()),
        out_specs=(field, field),
        check_vma=False,
    )
```

```python
import functools

import jax
import jax.numpy as jnp
from jax import lax
from jax.experimental import pallas as pl
from jax.experimental.pallas import tpu as pltpu
from jax.sharding import PartitionSpec as P

SUBSTEPS = 4
COARSE = 0.5
FINE = COARSE / SUBSTEPS
DRAG = 0.2
TILE = 8
LONG = 1 << 30
AXES = ("slab", "plane")

VMEM = pl.BlockSpec(memory_space=pltpu.VMEM)
HBM = pl.BlockSpec(memory_space=pltpu.HBM)
SMALL = pltpu.CompilerParams(vmem_limit_bytes=2 << 20)


def partner(index, count, second):
    other = ((index - 1) ^ 1) + 1 if second else index ^ 1
    return other if 0 <= other < count and (index or not second) else None


def swap_pairs(slabs, planes, along_slab, second):
    pairs = []
    for s in range(slabs):
        for p in range(planes):
            if along_slab:
                other = partner(s, slabs, second)
                target = (other, p) if other is not None else (s, p ^ 1 if (p ^ 1) < planes else None)
            else:
                other = partner(p, planes, second)
                rest = planes - 1 - p if planes % 2 == 0 else None
                target = (s, other if other is not None else rest)
            if target[1] is not None and target != (s, p):
                pairs.append((s * planes + p, target[0] * planes + target[1]))
    return pairs


def has_partner(index, count, second):
    even = index % 2 == 0
    up = jnp.logical_not(even) if second else even
    return jnp.where(up, index + 1 < count, index > 0)


def pin(arrays, space):
    return [pltpu.with_memory_space_constraint(a, space) for a in arrays]


def call(kernel, shapes, arrays, aliases=None, in_hbm=(), dtypes=None, scratch=(), to_hbm=(), weight=1):
    dtypes = dtypes or [jnp.float32] * len(shapes)
    out_shape = [pltpu.VMEM(s, t) for s, t in zip(shapes, dtypes)]
    out_shape += [pltpu.HBM(s, jnp.float32) for s in to_hbm]
    return pl.pallas_call(
        kernel,
        in_specs=[VMEM] * len(arrays) + [HBM] * len(in_hbm),
        out_specs=[VMEM] * len(shapes) + [HBM] * len(to_hbm),
        out_shape=out_shape,
        scratch_shapes=scratch,
        input_output_aliases=aliases or {},
        compiler_params=SMALL,
        cost_estimate=pl.CostEstimate(flops=weight, bytes_accessed=weight, transcendentals=0),
    )(*pin(arrays, pltpu.VMEM), *pin(in_hbm, pltpu.HBM))


def lookup(material, eroded, table):
    total = jnp.zeros(material.shape, jnp.float32)
    for index in range(table.shape[0]):
        total = jnp.where(material == index, table[index : index + 1, :], total)
    return total * (1 - eroded).astype(jnp.float32)


def run(start, rows, step=TILE):
    return pl.ds(start if isinstance(start, int) else pl.multiple_of(start, step), rows)


def layer(index, rows):
    return run(index * rows, rows, rows)


def sides(cx):
    slab = lax.axis_index("slab")
    even = slab % 2 == 0
    return jnp.where(even, cx - 1, 0), jnp.where(even, 0, cx - 1)


def plane_even():
    return lax.axis_index("plane") % 2 == 0


def start_copies(moves, sems):
    copies = [pltpu.make_async_copy(source, target, sems.at[i]) for i, (source, target) in enumerate(moves)]
    for copy in copies:
        copy.start()
    return copies


def open_kernel(
    cx, cy, u_hbm, material_hbm, eroded_hbm, table_hbm, damaged_hbm,
    a, b, ya, yb, u, material, eroded, table, damaged, scalars, edge, sems,
):
    moves = [(table_hbm, scalars), (material_hbm, material), (eroded_hbm, eroded)]
    moves += [(u_hbm.at[c], u.at[c]) for c in range(3)]
    copies = start_copies(moves + [(damaged_hbm, damaged)], sems)
    copies[0].wait()
    for index in range(table.shape[0]):
        table[index : index + 1, :] = jnp.full((1, table.shape[1]), scalars[index], jnp.float32)
    copies[1].wait()
    copies[2].wait()
    fa, fb = sides(cx)
    even = plane_even()
    for face, out in ((fa, a), (fb, b)):
        at = layer(face, cy)
        out[3] = lookup(material[at, :], eroded[at, :], table)
    for x in range(cx):
        top, end = slice(x * cy, x * cy + TILE), slice((x + 1) * cy - TILE, (x + 1) * cy)
        for i, cells in enumerate((material, eroded)):
            put_rows(even, x, i, cells[top, :], cells[end, :], edge.at[0], edge.at[1])
    for side, out in enumerate((ya, yb)):
        out[3] = lookup(edge[side, 0], edge[side, 1], table)
    for copy in copies[3:6]:
        copy.wait()
    for face, out in ((fa, a), (fb, b)):
        at = layer(face, cy)
        for c in range(3):
            out[c] = u[c, at, :]
    pack_rows(cx, cy, u, ya, yb)
    copies[6].wait()


def put_rows(even, x, c, first, last, ya, yb):
    first, last = first[0:1, :], last[TILE - 1 : TILE, :]
    ya[c, x : x + 1, :] = jnp.where(even, last, first)
    yb[c, x : x + 1, :] = jnp.where(even, first, last)


def advance(cx, cy, first, count, u, v, load, stiff, rate, u_out, v_out, halo=None, then=None, tiles=None):
    kx, ky_down, ky_up, kz_down, kz_up, total = stiff
    nz = u.shape[-1]
    row = lax.broadcasted_iota(jnp.int32, (TILE, nz), 0)
    even = plane_even()

    def tile(x, t):
        return run(x * cy + t * TILE, TILE)

    def clamp(x):
        return min(max(x, 0), cx - 1) if isinstance(x, int) else jnp.clip(x, 0, cx - 1)

    for i in range(count):
        x = first + i
        for t in tiles if tiles is not None else range(cy // TILE):
            at = tile(x, t)
            x_down, x_up = tile(clamp(x - 1), t), tile(clamp(x + 1), t)
            r = rate[at, :]
            for c in range(3):
                here = u[c, at, :]
                one, two = (h[c, pl.ds(x, 1), :] for h in halo) if halo else (here, here)
                if t > 0:
                    down = pltpu.roll(u[c, tile(x, t - 1), :], 1, 0)
                else:
                    down = jnp.where(even, two, one)
                if t < cy // TILE - 1:
                    up = pltpu.roll(u[c, tile(x, t + 1), :], TILE - 1, 0)
                else:
                    up = jnp.where(even, one, two)
                down = jnp.where(row == 0, down, pltpu.roll(here, 1, 0))
                up = jnp.where(row == TILE - 1, up, pltpu.roll(here, TILE - 1, 0))
                force = (kx[at, :] * u[c, x_down, :] + kx[tile(x + 1, t), :] * u[c, x_up, :]) - total[at, :] * here
                force = force + (ky_down[at, :] * down + ky_up[at, :] * up)
                force = force + (
                    kz_down[at, :] * pltpu.roll(here, 1, 1) + kz_up[at, :] * pltpu.roll(here, nz - 1, 1)
                )
                speed = v[c, at, :]
                speed = speed + r * (force + load[c, at, :] - DRAG * speed)
                v_out[c, at, :] = speed
                u_out[c, at, :] = here + r * speed
        if then is not None:
            then(i)


def rest_first(cx):
    return jnp.where(sides(cx)[1] == 0, 1, 0)


def advance_inner(cx, cy, u, v, load, stiff, rate, u_out, v_out):
    advance(cx, cy, sides(cx)[1], 1, u, v, load, stiff, rate, u_out, v_out)
    inner = range(1, cy // TILE - 1)
    advance(cx, cy, rest_first(cx), cx - 1, u, v, load, stiff, rate, u_out, v_out, tiles=inner)


def advance_outer(cx, cy, u, v, load, stiff, rate, u_out, v_out, halo, then=None):
    outer = sorted({0, cy // TILE - 1})
    advance(cx, cy, rest_first(cx), cx - 1, u, v, load, stiff, rate, u_out, v_out, halo, then, outer)


def edge_kernel(cx, cy, u, v, load, kx, kyd, kyu, kzd, kzu, total, rate, u_out, v_out):
    advance_inner(cx, cy, u, v, load, (kx, kyd, kyu, kzd, kzu, total), rate, u_out, v_out)


def rest_kernel(
    cx, cy, u1, v, u, load, kx, kyd, kyu, kzd, kzu, total, rate, ya, yb, u_out, v_out, ya_send, yb_send
):
    stiff = kx, kyd, kyu, kzd, kzu, total
    advance_outer(cx, cy, u, v, load, stiff, rate, u_out, v_out, (ya, yb))
    pack_rows(cx, cy, u_out, ya_send, yb_send)


def rest_kernel_plain(cx, cy, u1, v, u, load, kx, kyd, kyu, kzd, kzu, total, rate, ya, yb, u_out, v_out):
    stiff = kx, kyd, kyu, kzd, kzu, total
    advance_outer(cx, cy, u, v, load, stiff, rate, u_out, v_out, (ya, yb))


def last_inner(
    cx, cy, u, v, load, kx, kyd, kyu, kzd, kzu, total, rate, hb, kb, u_out, v_out, u_hbm, v_hbm, sems
):
    stiff = kx, kyd, kyu, kzd, kzu, total
    fa, fb = sides(cx)
    copies = []

    def send(x):
        at = run(x * cy + TILE, cy - 2 * TILE)
        for source, target in ((u_out, u_hbm), (v_out, v_hbm)):
            copy = pltpu.make_async_copy(source.at[:, at, :], target.at[:, at, :], sems.at[len(copies)])
            copy.start()
            copies.append(copy)

    advance(cx, cy, fb, 1, u, v, load, stiff, rate, u_out, v_out)
    fix_face(layer(fb, cy), u, rate, kb[...], lambda c: hb[c], u_out, v_out)
    send(fb)
    advance(cx, cy, 1, cx - 2, u, v, load, stiff, rate, u_out, v_out, then=lambda i: send(1 + i))
    advance(cx, cy, fa, 1, u, v, load, stiff, rate, u_out, v_out)
    for copy in copies:
        copy.wait()


def rest_kernel_first(
    cx, cy, u1, v1, kyd, kyu, total, u, v, load, kx, kzd, kzu, rate, ya, yb, ya_sent, yb_sent,
    u_out, v_out, kyd_out, kyu_out, total_out, k_low, k_high, sides_k,
):
    low, high = row_stiffness(ya_sent, yb_sent, ya, yb)
    sides_k[0], sides_k[1] = low, high
    row = lax.broadcasted_iota(jnp.int32, (TILE, u.shape[-1]), 0)
    face = sides(cx)[1]
    k_low[...] = jnp.where(row == 0, sides_k[0, pl.ds(face, 1), :], 0.0)
    k_high[...] = jnp.where(row == TILE - 1, sides_k[1, pl.ds(face, 1), :], 0.0)
    for x in range(cx):
        for start, edge, k, out in (
            (x * cy, 0, low, kyd_out),
            ((x + 1) * cy - TILE, TILE - 1, high, kyu_out),
        ):
            at = slice(start, start + TILE)
            extra = jnp.where(row == edge, k[x : x + 1, :], 0.0)
            out[at, :] += extra
            total_out[at, :] += extra
    stiff = kx, kyd_out, kyu_out, kzd, kzu, total_out
    advance_outer(cx, cy, u, v, load, stiff, rate, u_out, v_out, (ya, yb))


def pack_first(cx, cy, u_new, fine, ya_send, yb_send):
    pack_rows(cx, cy, u_new, ya_send, yb_send, fine)


def prepare_kernel(
    cx, cy, u, material, eroded, table, v, load, damaged,
    u_out, v_out, kx, kyd, kyu, kzd, kzu, total, coarse, fine, k_all,
):
    nz = u.shape[-1]
    row = lax.broadcasted_iota(jnp.int32, (TILE, nz), 0)
    lane = lax.broadcasted_iota(jnp.int32, (TILE, nz), 1)
    nothing = jnp.zeros((TILE, nz), jnp.float32)
    tiles = cy // TILE
    for start in range(0, cx * cy, TILE):
        at = slice(start, start + TILE)
        k_all[at, :] = lookup(material[at, :], eroded[at, :], table)
    for t in range(tiles):
        face = nothing
        for x in range(cx):
            start = x * cy + t * TILE
            at = slice(start, start + TILE)
            k = k_all[at, :]
            y_up = k_all[start + TILE : start + TILE + 1, :] if t < tiles - 1 else 0.0
            y_down = k_all[start - 1 : start, :] if t > 0 else 0.0
            y_up = jnp.minimum(k, jnp.where(row == TILE - 1, y_up, pltpu.roll(k, TILE - 1, 0)))
            y_down = jnp.minimum(k, jnp.where(row == 0, y_down, pltpu.roll(k, 1, 0)))
            z_up = jnp.minimum(k, jnp.where(lane == nz - 1, 0.0, pltpu.roll(k, nz - 1, 1)))
            z_down = jnp.minimum(k, jnp.where(lane == 0, 0.0, pltpu.roll(k, 1, 1)))
            face_up = jnp.minimum(k, k_all[start + cy : start + cy + TILE, :]) if x < cx - 1 else nothing
            for out, value in ((kx, face), (kyu, y_up), (kyd, y_down), (kzu, z_up), (kzd, z_down)):
                out[at, :] = value
            total[at, :] = ((face + face_up) + (y_up + y_down)) + (z_up + z_down)
            face = face_up
    kx[cx * cy : (cx + 1) * cy, :] = jnp.zeros((cy, nz), jnp.float32)
    for x in range(cx):
        at = slice(x * cy, (x + 1) * cy)
        hit = damaged[at, :] == 1
        coarse[at, :] = jnp.where(hit, FINE, COARSE)
        fine[at, :] = jnp.where(hit, FINE, 0.0)
    stiff = kx, kyd, kyu, kzd, kzu, total
    advance_inner(cx, cy, u, v, load, stiff, coarse, u_out, v_out)


def fix_face(at, u, rate, k, halo, u_new, v_new, put=None):
    r = rate[at, :]
    for c in range(3):
        push = r * (k * (halo(c) - u[c, at, :]))
        v_new[c, at, :] += push
        moved = u_new[c, at, :] + r * push
        u_new[c, at, :] = moved
        if put is not None:
            put(c, moved)


def fix_rows(cy, x, u, rate, k_low, k_high, ya, yb, u_new, v_new):
    even = plane_even()
    for start, k, flip in ((x * cy, k_low, False), ((x + 1) * cy - TILE, k_high, True)):
        at = pl.ds(pl.multiple_of(start, TILE), TILE)
        r = rate[at, :]
        for c in range(3):
            one, two = ya[c, pl.ds(x, 1), :], yb[c, pl.ds(x, 1), :]
            halo = jnp.where(even, one, two) if flip else jnp.where(even, two, one)
            push = r * (k[...] * (halo - u[c, at, :]))
            v_new[c, at, :] += push
            u_new[c, at, :] += r * push


def pack_rows(cx, cy, u_new, ya_send, yb_send, cells=None):
    even = plane_even()
    for c in range(3 if cells is None else 4):
        for x in range(cx):
            top, end = slice(x * cy, x * cy + TILE), slice((x + 1) * cy - TILE, (x + 1) * cy)
            if c < 3:
                first, last = u_new[c, top, :], u_new[c, end, :]
            else:
                first, last = cells[top, :], cells[end, :]
            put_rows(even, x, c, first, last, ya_send, yb_send)


def flag(axis, second):
    return has_partner(lax.axis_index(axis), lax.axis_size(axis), second).astype(jnp.float32)


def face_stiffness(sent, received, second):
    return jnp.minimum(sent[3], received[3]) * flag("slab", second)


def row_stiffness(ya_sent, yb_sent, ya, yb):
    even = plane_even()
    k_a = jnp.minimum(ya_sent[3], ya[3]) * flag("plane", False)
    k_b = jnp.minimum(yb_sent[3], yb[3]) * flag("plane", True)
    return jnp.where(even, k_b, k_a), jnp.where(even, k_a, k_b)


def fix_b_first(cx, cy, u1, v1, u, rate, hb, ya, yb, b_sent, k_low, k_high, u_new, v_new, send, kb):
    kb[...] = face_stiffness(b_sent, hb, True)
    fix_b(cx, cy, u1, v1, u, rate, hb, ya, yb, kb, k_low, k_high, u_new, v_new, send)


def fix_b(cx, cy, u1, v1, u, rate, hb, ya, yb, kb, k_low, k_high, u_new, v_new, send=None):
    face = sides(cx)[1]
    fix_rows(cy, face, u, rate, k_low, k_high, ya, yb, u_new, v_new)

    def put(c, moved):
        if send is not None:
            send[c] = moved

    fix_face(layer(face, cy), u, rate, kb[...], lambda c: hb[c], u_new, v_new, put)


def put_face(cy, send):
    def put(c, moved):
        send[c * cy : (c + 1) * cy, :] = moved

    return put


def put_halos(cy, x, ya, yb, send):
    for c in range(4):
        if c < ya.shape[0]:
            rows = halo_rows(ya, yb, c, x)
        else:
            rows = [jnp.zeros((1, send.shape[1]), jnp.float32)] * 2
        for side in range(2):
            at = 3 * cy + 4 * side + c
            send[at : at + 1, :] = rows[side]


def halo_rows(ya, yb, c, x):
    even = plane_even()
    one, two = ya[c, pl.ds(x, 1), :], yb[c, pl.ds(x, 1), :]
    return jnp.where(even, two, one), jnp.where(even, one, two)


def coarse_of(fine):
    return COARSE + (FINE - COARSE) / FINE * fine


def correct(cx, cy, step, rate, ha, ya, yb, kyd, kyu, old_ya, old_yb, state, u_new, v_new, state_out):
    face = sides(cx)[0]
    row = lax.broadcasted_iota(jnp.int32, (TILE, rate.shape[1]), 0)
    for side in range(2):
        def sent(f, base=3 * cy + 4 * side):
            return ha[base + f : base + f + 1, :]

        def kept(f, side=side):
            return state[side, f : f + 1, :]

        if step == 1:
            k = jnp.minimum(halo_rows(old_ya, old_yb, 3, face)[side], sent(3)) * flag("slab", False)
            mine = halo_rows(ya, yb, 3, face)[side]
            other = jnp.zeros_like(mine)
            scale = coarse_of(mine) * coarse_of(mine) * k
        else:
            k, mine = kept(9), kept(10)
            other = sent(3) if step == 2 else kept(11)
            scale = mine * mine * k
            pace = coarse_of(other) if step == 2 else other
            pace = pace * pace * k
        start = face * cy if side == 0 else (face + 1) * cy - TILE
        at = pl.ds(pl.multiple_of(start, TILE), TILE)
        edge_k = jnp.where(row == (0 if side == 0 else TILE - 1), (kyd if side == 0 else kyu)[at, :], 0.0)
        r = rate[at, :]
        for c in range(3):
            if step == 1:
                before, across = halo_rows(old_ya, old_yb, c, face)[side], sent(c)
            else:
                before = kept(c)
                across = sent(c) + pace * (kept(3 + c) - kept(6 + c))
            late = scale * (across - before)
            push = r * (edge_k * late)
            v_new[c, at, :] += push
            u_new[c, at, :] += r * push
            if state_out is not None:
                now = halo_rows(ya, yb, c, face)[side] + late
                for f, value in ((c, now), (3 + c, before), (6 + c, across)):
                    state_out[side, f : f + 1, :] = value
        if state_out is not None:
            for f, value in ((9, k), (10, mine), (11, other)):
                state_out[side, f : f + 1, :] = value


def fix_a_first(cx, cy, u1, v1, u, rate, ha, a_sent, ya, yb, u_new, v_new, send, ka):
    ka[...] = face_stiffness(a_sent, ha, False)
    face = sides(cx)[0]
    put_halos(cy, face, ya, yb, send)
    fix_face(layer(face, cy), u, rate, ka[...], lambda c: ha[c], u_new, v_new, put_face(cy, send))


def fix_a_second(
    cx, cy, u1, v1, u, rate, ha, ka, ya, yb, kyd, kyu, old_ya, old_yb, u_new, v_new, send, state_out
):
    correct(cx, cy, 1, rate, ha, ya, yb, kyd, kyu, old_ya, old_yb, None, u_new, v_new, state_out)
    finish_a(cx, cy, u, rate, ha, ka, ya, yb, u_new, v_new, send)


def fix_a_third(
    cx, cy, u1, v1, u, rate, ha, ka, ya, yb, kyd, kyu, state, u_new, v_new, send, ya_send, yb_send
):
    correct(cx, cy, 2, rate, ha, ya, yb, kyd, kyu, None, None, state, u_new, v_new, None)
    close_face(cx, cy, u, rate, ha, ka, u_new, v_new, send)
    pack_rows(cx, cy, u_new, ya_send, yb_send)


def finish_a(cx, cy, u, rate, ha, ka, ya, yb, u_new, v_new, send):
    put_halos(cy, sides(cx)[0], ya, yb, send)
    close_face(cx, cy, u, rate, ha, ka, u_new, v_new, send)


def close_face(cx, cy, u, rate, ha, ka, u_new, v_new, send):
    at = layer(sides(cx)[0], cy)
    fix_face(at, u, rate, ka[...], lambda c: ha[c * cy : (c + 1) * cy, :], u_new, v_new, put_face(cy, send))


def hand_on(*refs):
    del refs


def after(array, other):
    return call(hand_on, [array.shape], (array, other), {0: 0})[0]


def last_outer(
    cx, cy, u1, v1, u, rate, ha, ka, ya, yb, kyd, kyu, u_in, v_in, u_new, v_new, u_hbm, v_hbm, sems
):
    rows = cx * cy
    fa = sides(cx)[0]
    row = lax.broadcasted_iota(jnp.int32, (TILE, u.shape[-1]), 0)
    copies = []

    def send(start, size):
        at = run(start, size)
        for source, target in ((u_new, u_hbm), (v_new, v_hbm)):
            copy = pltpu.make_async_copy(source.at[:, at, :], target.at[:, at, :], sems.at[len(copies)])
            copy.start()
            copies.append(copy)

    fix_face(layer(fa, cy), u, rate, ka[...], lambda c: ha[c * cy : (c + 1) * cy, :], u_new, v_new)
    send(fa * cy + TILE, cy - 2 * TILE)
    for x in range(cx):
        for side, (start, edge, stiff) in enumerate(((x * cy, 0, kyd), ((x + 1) * cy - TILE, TILE - 1, kyu))):
            at = slice(start, start + TILE)
            k = jnp.where(row == edge, stiff[at, :], 0.0)
            r = rate[at, :]
            for c in range(3):
                push = r * (k * (halo_rows(ya, yb, c, x)[side] - u[c, at, :]))
                v_new[c, at, :] += push
                u_new[c, at, :] += r * push
            if side == 0:
                begin = max(start - TILE, 0)
                send(begin, start + TILE - begin)
    send(rows - TILE, TILE)
    for copy in copies:
        copy.wait()


def per_device(displacement, velocity, body_load, damaged, eroded, material, stiff_table):
    _, cx, cy, nz = displacement.shape
    rows = cx * cy
    slabs, planes = lax.axis_size("slab"), lax.axis_size("plane")
    xa = swap_pairs(slabs, planes, True, False)
    xb = swap_pairs(slabs, planes, True, True)
    pa = swap_pairs(slabs, planes, False, False)
    pb = swap_pairs(slabs, planes, False, True)

    field, face, side, cells = (3, rows, nz), (3, cy, nz), (3, cx, nz), (rows, nz)
    u = displacement.reshape(field)
    v = velocity.reshape(field)
    load = body_load.reshape(field)
    damaged, eroded, material = (a.reshape(cells) for a in (damaged, eroded, material))

    def bind(kernel):
        return functools.partial(kernel, cx, cy)

    table_shape = (stiff_table.shape[0], nz)
    a, b, ya, yb, u, material, eroded, table, damaged = call(
        bind(open_kernel),
        [(4, cy, nz)] * 2 + [(4, cx, nz)] * 2 + [field, cells, cells, table_shape, cells],
        (),
        in_hbm=(u, material, eroded, stiff_table, damaged),
        dtypes=[jnp.float32] * 5 + [jnp.int32] * 2 + [jnp.float32, jnp.int32],
        scratch=[
            pltpu.SMEM(stiff_table.shape, jnp.float32),
            pltpu.VMEM((2, 2, cx, nz), jnp.int32),
            pltpu.SemaphoreType.DMA((7,)),
        ],
    )
    both = {0: 0, 1: 1}
    for sub in range(SUBSTEPS):
        last = sub == SUBSTEPS - 1
        hb = lax.ppermute(b, AXES, xb)
        if sub == 0:
            yb = after(yb, b)
        if last:
            yb = after(yb, a)
        hyb = lax.ppermute(yb, AXES, pb)
        if sub == 0:
            a = after(a, yb)
        ha = lax.ppermute(a, AXES, xa)
        hya = lax.ppermute(ya, AXES, pa)
        if sub == 0:
            u_new, v_new, kx, kyd, kyu, kzd, kzu, total, coarse, fine = call(
                bind(prepare_kernel),
                [field] * 2 + [((cx + 1) * cy, nz)] + [cells] * 7,
                (u, material, eroded, table, v, load, damaged),
                scratch=[pltpu.VMEM(cells, jnp.float32)],
            )
            rate = coarse
            u_new, v, kyd, kyu, total, k_low, k_high = call(
                bind(rest_kernel_first),
                [field, field] + [cells] * 3 + [(TILE, nz)] * 2,
                (u_new, v_new, kyd, kyu, total, u, v, load, kx, kzd, kzu, rate, hya, hyb, ya, yb),
                {i: i for i in range(5)},
                scratch=[pltpu.VMEM((2, cx, nz), jnp.float32)],
            )
            u_new, v, b_next, kb = call(
                bind(fix_b_first),
                [field, field, face, (cy, nz)],
                (u_new, v, u, rate, hb, hya, hyb, b, k_low, k_high),
                both,
                weight=LONG,
            )
            sides_next = call(bind(pack_first), [(4, cx, nz)] * 2, (u_new, fine))
        elif not last:
            rate = fine
            stiff = kx, kyd, kyu, kzd, kzu, total
            u_new, v = call(bind(edge_kernel), [field, field], (u, v, load, *stiff, rate), {1: 1})
            u_new, v, b_next = call(
                bind(fix_b),
                [field, field, face],
                (u_new, v, u, rate, hb, hya, hyb, kb, k_low, k_high),
                both,
                weight=LONG,
            )
            packs = sub < SUBSTEPS - 2
            u_new, v, *sides_next = call(
                bind(rest_kernel if packs else rest_kernel_plain),
                [field, field] + ([side, side] if packs else []),
                (u_new, v, u, load, *stiff, rate, hya, hyb),
                both,
            )
        else:
            break
        b = b_next
        face_and_halos, state_shape = (3 * cy + TILE, nz), (2, 16, nz)
        if sub == 0:
            u_new, v, a, ka = call(
                bind(fix_a_first),
                [field, field, face_and_halos, (cy, nz)],
                (u_new, v, u, rate, ha, a, hya, hyb),
                both,
            )
            old = hya, hyb
        elif sub == 1:
            u_new, v, a, state = call(
                bind(fix_a_second),
                [field, field, face_and_halos, state_shape],
                (u_new, v, u, rate, ha, ka, hya, hyb, kyd, kyu, *old),
                both,
            )
        else:
            u_new, v, a, *sides_next = call(
                bind(fix_a_third),
                [field, field, (3 * cy, nz), side, side],
                (u_new, v, u, rate, ha, ka, hya, hyb, kyd, kyu, state),
                both,
            )
        u = u_new
        ya, yb = sides_next
    u_new, v, *out = call(
        bind(last_inner),
        [field, field],
        (u, v, load, *stiff, fine, hb, kb),
        {1: 1},
        scratch=[pltpu.SemaphoreType.DMA((2 * (cx - 1),))],
        to_hbm=[field, field],
    )
    out = call(
        bind(last_outer),
        [field, field],
        (u_new, v, u, fine, ha, ka, hya, hyb, kyd, kyu),
        {0: 0, 1: 1, 10: 2, 11: 3},
        in_hbm=out,
        scratch=[pltpu.SemaphoreType.DMA((2 * (cx + 2),))],
        to_hbm=[field, field],
    )
    return out[2].reshape(displacement.shape), out[3].reshape(displacement.shape)


def solution(mesh):
    field, cells = P(None, "slab", "plane", None), P("slab", "plane", None)
    return jax.shard_map(
        per_device,
        mesh=mesh,
        in_specs=(field, field, field, cells, cells, cells, P()),
        out_specs=(field, field),
        check_vma=False,
    )
```

```python
import functools

import jax
import jax.numpy as jnp
from jax import lax
from jax.experimental import pallas as pl
from jax.experimental.pallas import tpu as pltpu
from jax.sharding import PartitionSpec as P

SUBSTEPS = 4
COARSE = 0.5
FINE = COARSE / SUBSTEPS
DRAG = 0.2
TILE = 8
LONG = 1 << 30
AXES = ("slab", "plane")

VMEM = pl.BlockSpec(memory_space=pltpu.VMEM)
HBM = pl.BlockSpec(memory_space=pltpu.HBM)
SMALL = pltpu.CompilerParams(vmem_limit_bytes=2 << 20)


def partner(index, count, second):
    other = ((index - 1) ^ 1) + 1 if second else index ^ 1
    return other if 0 <= other < count and (index or not second) else None


def swap_pairs(slabs, planes, along_slab, second):
    pairs = []
    for s in range(slabs):
        for p in range(planes):
            if along_slab:
                other = partner(s, slabs, second)
                target = (other, p) if other is not None else (s, p ^ 1 if (p ^ 1) < planes else None)
            else:
                other = partner(p, planes, second)
                rest = planes - 1 - p if planes % 2 == 0 else None
                target = (s, other if other is not None else rest)
            if target[1] is not None and target != (s, p):
                pairs.append((s * planes + p, target[0] * planes + target[1]))
    return pairs


def has_partner(index, count, second):
    even = index % 2 == 0
    up = jnp.logical_not(even) if second else even
    return jnp.where(up, index + 1 < count, index > 0)


def pin(arrays, space):
    return [pltpu.with_memory_space_constraint(a, space) for a in arrays]


def call(kernel, shapes, arrays, aliases=None, in_hbm=(), dtypes=None, scratch=(), to_hbm=(), weight=1):
    dtypes = dtypes or [jnp.float32] * len(shapes)
    out_shape = [pltpu.VMEM(s, t) for s, t in zip(shapes, dtypes)]
    out_shape += [pltpu.HBM(s, jnp.float32) for s in to_hbm]
    return pl.pallas_call(
        kernel,
        in_specs=[VMEM] * len(arrays) + [HBM] * len(in_hbm),
        out_specs=[VMEM] * len(shapes) + [HBM] * len(to_hbm),
        out_shape=out_shape,
        scratch_shapes=scratch,
        input_output_aliases=aliases or {},
        compiler_params=SMALL,
        cost_estimate=pl.CostEstimate(flops=weight, bytes_accessed=weight, transcendentals=0),
    )(*pin(arrays, pltpu.VMEM), *pin(in_hbm, pltpu.HBM))


def lookup(material, eroded, table):
    total = jnp.zeros(material.shape, jnp.float32)
    for index in range(table.shape[0]):
        total = jnp.where(material == index, table[index : index + 1, :], total)
    return total * (1 - eroded).astype(jnp.float32)


def run(start, rows, step=TILE):
    return pl.ds(start if isinstance(start, int) else pl.multiple_of(start, step), rows)


def layer(index, rows):
    return run(index * rows, rows, rows)


def sides(cx):
    slab = lax.axis_index("slab")
    even = slab % 2 == 0
    return jnp.where(even, cx - 1, 0), jnp.where(even, 0, cx - 1)


def plane_even():
    return lax.axis_index("plane") % 2 == 0


def start_copies(moves, sems):
    copies = [pltpu.make_async_copy(source, target, sems.at[i]) for i, (source, target) in enumerate(moves)]
    for copy in copies:
        copy.start()
    return copies


def open_b(
    cx, cy, u_hbm, material_hbm, eroded_hbm, table_hbm, damaged_hbm, b, table, damaged, scalars, cells, sems
):
    at = layer(sides(cx)[1], cy)
    moves = [(table_hbm, scalars), (material_hbm.at[at, :], cells.at[0]), (eroded_hbm.at[at, :], cells.at[1])]
    moves += [(u_hbm.at[:, at, :], b.at[pl.ds(0, 3)]), (damaged_hbm, damaged)]
    copies = start_copies(moves, sems)
    copies[0].wait()
    for index in range(table.shape[0]):
        table[index : index + 1, :] = jnp.full((1, table.shape[1]), scalars[index], jnp.float32)
    copies[1].wait()
    copies[2].wait()
    b[3] = lookup(cells[0], cells[1], table)
    copies[3].wait()
    copies[4].wait()


def open_rest(cx, cy, b_sent, u, material, eroded, table, a, ya, yb, edge):
    even = plane_even()
    at = layer(sides(cx)[0], cy)
    a[3] = lookup(material[at, :], eroded[at, :], table)
    for c in range(3):
        a[c] = u[c, at, :]
    for x in range(cx):
        top, end = slice(x * cy, x * cy + TILE), slice((x + 1) * cy - TILE, (x + 1) * cy)
        for i, cells in enumerate((material, eroded)):
            put_rows(even, x, i, cells[top, :], cells[end, :], edge.at[0], edge.at[1])
    for side, out in enumerate((ya, yb)):
        out[3] = lookup(edge[side, 0], edge[side, 1], table)
    pack_rows(cx, cy, u, ya, yb)


def put_rows(even, x, c, first, last, ya, yb):
    first, last = first[0:1, :], last[TILE - 1 : TILE, :]
    ya[c, x : x + 1, :] = jnp.where(even, last, first)
    yb[c, x : x + 1, :] = jnp.where(even, first, last)


def advance(cx, cy, first, count, u, v, load, stiff, rate, u_out, v_out, halo=None, then=None, tiles=None):
    kx, ky_down, ky_up, kz_down, kz_up, total = stiff
    nz = u.shape[-1]
    row = lax.broadcasted_iota(jnp.int32, (TILE, nz), 0)
    even = plane_even()

    def tile(x, t):
        return run(x * cy + t * TILE, TILE)

    def clamp(x):
        return min(max(x, 0), cx - 1) if isinstance(x, int) else jnp.clip(x, 0, cx - 1)

    for i in range(count):
        x = first + i
        for t in tiles if tiles is not None else range(cy // TILE):
            at = tile(x, t)
            x_down, x_up = tile(clamp(x - 1), t), tile(clamp(x + 1), t)
            r = rate[at, :]
            for c in range(3):
                here = u[c, at, :]
                one, two = (h[c, pl.ds(x, 1), :] for h in halo) if halo else (here, here)
                if t > 0:
                    down = pltpu.roll(u[c, tile(x, t - 1), :], 1, 0)
                else:
                    down = jnp.where(even, two, one)
                if t < cy // TILE - 1:
                    up = pltpu.roll(u[c, tile(x, t + 1), :], TILE - 1, 0)
                else:
                    up = jnp.where(even, one, two)
                down = jnp.where(row == 0, down, pltpu.roll(here, 1, 0))
                up = jnp.where(row == TILE - 1, up, pltpu.roll(here, TILE - 1, 0))
                force = (kx[at, :] * u[c, x_down, :] + kx[tile(x + 1, t), :] * u[c, x_up, :]) - total[at, :] * here
                force = force + (ky_down[at, :] * down + ky_up[at, :] * up)
                force = force + (
                    kz_down[at, :] * pltpu.roll(here, 1, 1) + kz_up[at, :] * pltpu.roll(here, nz - 1, 1)
                )
                speed = v[c, at, :]
                speed = speed + r * (force + load[c, at, :] - DRAG * speed)
                v_out[c, at, :] = speed
                u_out[c, at, :] = here + r * speed
        if then is not None:
            then(i)


def rest_first(cx):
    return jnp.where(sides(cx)[1] == 0, 1, 0)


def advance_inner(cx, cy, u, v, load, stiff, rate, u_out, v_out):
    advance(cx, cy, sides(cx)[1], 1, u, v, load, stiff, rate, u_out, v_out)
    inner = range(1, cy // TILE - 1)
    advance(cx, cy, rest_first(cx), cx - 1, u, v, load, stiff, rate, u_out, v_out, tiles=inner)


def advance_outer(cx, cy, u, v, load, stiff, rate, u_out, v_out, halo, then=None):
    outer = sorted({0, cy // TILE - 1})
    advance(cx, cy, rest_first(cx), cx - 1, u, v, load, stiff, rate, u_out, v_out, halo, then, outer)


def edge_kernel(cx, cy, u, v, load, kx, kyd, kyu, kzd, kzu, total, rate, u_out, v_out):
    advance_inner(cx, cy, u, v, load, (kx, kyd, kyu, kzd, kzu, total), rate, u_out, v_out)


def rest_kernel(
    cx, cy, u1, v, u, load, kx, kyd, kyu, kzd, kzu, total, rate, ya, yb, u_out, v_out, ya_send, yb_send
):
    stiff = kx, kyd, kyu, kzd, kzu, total
    advance_outer(cx, cy, u, v, load, stiff, rate, u_out, v_out, (ya, yb))
    pack_rows(cx, cy, u_out, ya_send, yb_send)


def rest_kernel_plain(cx, cy, u1, v, u, load, kx, kyd, kyu, kzd, kzu, total, rate, ya, yb, u_out, v_out):
    stiff = kx, kyd, kyu, kzd, kzu, total
    advance_outer(cx, cy, u, v, load, stiff, rate, u_out, v_out, (ya, yb))


def last_inner(
    cx, cy, u, v, load, kx, kyd, kyu, kzd, kzu, total, rate, hb, kb, u_out, v_out, u_hbm, v_hbm, sems
):
    stiff = kx, kyd, kyu, kzd, kzu, total
    fa, fb = sides(cx)
    copies = []

    def send(x):
        at = run(x * cy + TILE, cy - 2 * TILE)
        for source, target in ((u_out, u_hbm), (v_out, v_hbm)):
            copy = pltpu.make_async_copy(source.at[:, at, :], target.at[:, at, :], sems.at[len(copies)])
            copy.start()
            copies.append(copy)

    advance(cx, cy, fb, 1, u, v, load, stiff, rate, u_out, v_out)
    fix_face(layer(fb, cy), u, rate, kb[...], lambda c: hb[c], u_out, v_out)
    send(fb)
    advance(cx, cy, 1, cx - 2, u, v, load, stiff, rate, u_out, v_out, then=lambda i: send(1 + i))
    advance(cx, cy, fa, 1, u, v, load, stiff, rate, u_out, v_out)
    for copy in copies:
        copy.wait()


def rest_kernel_first(
    cx, cy, u1, v1, kyd, kyu, total, u, v, load, kx, kzd, kzu, rate, ya, yb, ya_sent, yb_sent,
    u_out, v_out, kyd_out, kyu_out, total_out, k_low, k_high, sides_k,
):
    low, high = row_stiffness(ya_sent, yb_sent, ya, yb)
    sides_k[0], sides_k[1] = low, high
    row = lax.broadcasted_iota(jnp.int32, (TILE, u.shape[-1]), 0)
    face = sides(cx)[1]
    k_low[...] = jnp.where(row == 0, sides_k[0, pl.ds(face, 1), :], 0.0)
    k_high[...] = jnp.where(row == TILE - 1, sides_k[1, pl.ds(face, 1), :], 0.0)
    for x in range(cx):
        for start, edge, k, out in (
            (x * cy, 0, low, kyd_out),
            ((x + 1) * cy - TILE, TILE - 1, high, kyu_out),
        ):
            at = slice(start, start + TILE)
            extra = jnp.where(row == edge, k[x : x + 1, :], 0.0)
            out[at, :] += extra
            total_out[at, :] += extra
    stiff = kx, kyd_out, kyu_out, kzd, kzu, total_out
    advance_outer(cx, cy, u, v, load, stiff, rate, u_out, v_out, (ya, yb))


def pack_first(cx, cy, u_new, fine, ya_send, yb_send):
    pack_rows(cx, cy, u_new, ya_send, yb_send, fine)


def prepare_kernel(
    cx, cy, u, material, eroded, table, v, load, damaged,
    u_out, v_out, kx, kyd, kyu, kzd, kzu, total, coarse, fine, k_all,
):
    nz = u.shape[-1]
    row = lax.broadcasted_iota(jnp.int32, (TILE, nz), 0)
    lane = lax.broadcasted_iota(jnp.int32, (TILE, nz), 1)
    nothing = jnp.zeros((TILE, nz), jnp.float32)
    tiles = cy // TILE
    for start in range(0, cx * cy, TILE):
        at = slice(start, start + TILE)
        k_all[at, :] = lookup(material[at, :], eroded[at, :], table)
    for t in range(tiles):
        face = nothing
        for x in range(cx):
            start = x * cy + t * TILE
            at = slice(start, start + TILE)
            k = k_all[at, :]
            y_up = k_all[start + TILE : start + TILE + 1, :] if t < tiles - 1 else 0.0
            y_down = k_all[start - 1 : start, :] if t > 0 else 0.0
            y_up = jnp.minimum(k, jnp.where(row == TILE - 1, y_up, pltpu.roll(k, TILE - 1, 0)))
            y_down = jnp.minimum(k, jnp.where(row == 0, y_down, pltpu.roll(k, 1, 0)))
            z_up = jnp.minimum(k, jnp.where(lane == nz - 1, 0.0, pltpu.roll(k, nz - 1, 1)))
            z_down = jnp.minimum(k, jnp.where(lane == 0, 0.0, pltpu.roll(k, 1, 1)))
            face_up = jnp.minimum(k, k_all[start + cy : start + cy + TILE, :]) if x < cx - 1 else nothing
            for out, value in ((kx, face), (kyu, y_up), (kyd, y_down), (kzu, z_up), (kzd, z_down)):
                out[at, :] = value
            total[at, :] = ((face + face_up) + (y_up + y_down)) + (z_up + z_down)
            face = face_up
    kx[cx * cy : (cx + 1) * cy, :] = jnp.zeros((cy, nz), jnp.float32)
    for x in range(cx):
        at = slice(x * cy, (x + 1) * cy)
        hit = damaged[at, :] == 1
        coarse[at, :] = jnp.where(hit, FINE, COARSE)
        fine[at, :] = jnp.where(hit, FINE, 0.0)
    stiff = kx, kyd, kyu, kzd, kzu, total
    advance_inner(cx, cy, u, v, load, stiff, coarse, u_out, v_out)


def fix_face(at, u, rate, k, halo, u_new, v_new, put=None):
    r = rate[at, :]
    for c in range(3):
        push = r * (k * (halo(c) - u[c, at, :]))
        v_new[c, at, :] += push
        moved = u_new[c, at, :] + r * push
        u_new[c, at, :] = moved
        if put is not None:
            put(c, moved)


def fix_rows(cy, x, u, rate, k_low, k_high, ya, yb, u_new, v_new):
    even = plane_even()
    for start, k, flip in ((x * cy, k_low, False), ((x + 1) * cy - TILE, k_high, True)):
        at = pl.ds(pl.multiple_of(start, TILE), TILE)
        r = rate[at, :]
        for c in range(3):
            one, two = ya[c, pl.ds(x, 1), :], yb[c, pl.ds(x, 1), :]
            halo = jnp.where(even, one, two) if flip else jnp.where(even, two, one)
            push = r * (k[...] * (halo - u[c, at, :]))
            v_new[c, at, :] += push
            u_new[c, at, :] += r * push


def pack_rows(cx, cy, u_new, ya_send, yb_send, cells=None):
    even = plane_even()
    for c in range(3 if cells is None else 4):
        for x in range(cx):
            top, end = slice(x * cy, x * cy + TILE), slice((x + 1) * cy - TILE, (x + 1) * cy)
            if c < 3:
                first, last = u_new[c, top, :], u_new[c, end, :]
            else:
                first, last = cells[top, :], cells[end, :]
            put_rows(even, x, c, first, last, ya_send, yb_send)


def flag(axis, second):
    return has_partner(lax.axis_index(axis), lax.axis_size(axis), second).astype(jnp.float32)


def face_stiffness(sent, received, second):
    return jnp.minimum(sent[3], received[3]) * flag("slab", second)


def row_stiffness(ya_sent, yb_sent, ya, yb):
    even = plane_even()
    k_a = jnp.minimum(ya_sent[3], ya[3]) * flag("plane", False)
    k_b = jnp.minimum(yb_sent[3], yb[3]) * flag("plane", True)
    return jnp.where(even, k_b, k_a), jnp.where(even, k_a, k_b)


def fix_b_first(cx, cy, u1, v1, u, rate, hb, ya, yb, b_sent, k_low, k_high, u_new, v_new, send, kb):
    kb[...] = face_stiffness(b_sent, hb, True)
    fix_b(cx, cy, u1, v1, u, rate, hb, ya, yb, kb, k_low, k_high, u_new, v_new, send)


def fix_b(cx, cy, u1, v1, u, rate, hb, ya, yb, kb, k_low, k_high, u_new, v_new, send=None):
    face = sides(cx)[1]
    fix_rows(cy, face, u, rate, k_low, k_high, ya, yb, u_new, v_new)

    def put(c, moved):
        if send is not None:
            send[c] = moved

    fix_face(layer(face, cy), u, rate, kb[...], lambda c: hb[c], u_new, v_new, put)


def put_face(cy, send):
    def put(c, moved):
        send[c * cy : (c + 1) * cy, :] = moved

    return put


def put_halos(cy, x, ya, yb, send):
    for c in range(4):
        if c < ya.shape[0]:
            rows = halo_rows(ya, yb, c, x)
        else:
            rows = [jnp.zeros((1, send.shape[1]), jnp.float32)] * 2
        for side in range(2):
            at = 3 * cy + 4 * side + c
            send[at : at + 1, :] = rows[side]


def halo_rows(ya, yb, c, x):
    even = plane_even()
    one, two = ya[c, pl.ds(x, 1), :], yb[c, pl.ds(x, 1), :]
    return jnp.where(even, two, one), jnp.where(even, one, two)


def coarse_of(fine):
    return COARSE + (FINE - COARSE) / FINE * fine


def correct(cx, cy, step, rate, ha, ya, yb, kyd, kyu, old_ya, old_yb, state, u_new, v_new, state_out):
    face = sides(cx)[0]
    row = lax.broadcasted_iota(jnp.int32, (TILE, rate.shape[1]), 0)
    for side in range(2):
        def sent(f, base=3 * cy + 4 * side):
            return ha[base + f : base + f + 1, :]

        def kept(f, side=side):
            return state[side, f : f + 1, :]

        if step == 1:
            k = jnp.minimum(halo_rows(old_ya, old_yb, 3, face)[side], sent(3)) * flag("slab", False)
            mine = halo_rows(ya, yb, 3, face)[side]
            other = jnp.zeros_like(mine)
            scale = coarse_of(mine) * coarse_of(mine) * k
        else:
            k, mine = kept(9), kept(10)
            other = sent(3) if step == 2 else kept(11)
            scale = mine * mine * k
            pace = coarse_of(other) if step == 2 else other
            pace = pace * pace * k
        start = face * cy if side == 0 else (face + 1) * cy - TILE
        at = pl.ds(pl.multiple_of(start, TILE), TILE)
        edge_k = jnp.where(row == (0 if side == 0 else TILE - 1), (kyd if side == 0 else kyu)[at, :], 0.0)
        r = rate[at, :]
        for c in range(3):
            if step == 1:
                before, across = halo_rows(old_ya, old_yb, c, face)[side], sent(c)
            else:
                before = kept(c)
                across = sent(c) + pace * (kept(3 + c) - kept(6 + c))
            late = scale * (across - before)
            push = r * (edge_k * late)
            v_new[c, at, :] += push
            u_new[c, at, :] += r * push
            if state_out is not None:
                now = halo_rows(ya, yb, c, face)[side] + late
                for f, value in ((c, now), (3 + c, before), (6 + c, across)):
                    state_out[side, f : f + 1, :] = value
        if state_out is not None:
            for f, value in ((9, k), (10, mine), (11, other)):
                state_out[side, f : f + 1, :] = value


def fix_a_first(cx, cy, u1, v1, u, rate, ha, a_sent, ya, yb, u_new, v_new, send, ka):
    ka[...] = face_stiffness(a_sent, ha, False)
    face = sides(cx)[0]
    put_halos(cy, face, ya, yb, send)
    fix_face(layer(face, cy), u, rate, ka[...], lambda c: ha[c], u_new, v_new, put_face(cy, send))


def fix_a_second(
    cx, cy, u1, v1, u, rate, ha, ka, ya, yb, kyd, kyu, old_ya, old_yb, u_new, v_new, send, state_out
):
    correct(cx, cy, 1, rate, ha, ya, yb, kyd, kyu, old_ya, old_yb, None, u_new, v_new, state_out)
    finish_a(cx, cy, u, rate, ha, ka, ya, yb, u_new, v_new, send)


def fix_a_third(
    cx, cy, u1, v1, u, rate, ha, ka, ya, yb, kyd, kyu, state, u_new, v_new, send, ya_send, yb_send
):
    correct(cx, cy, 2, rate, ha, ya, yb, kyd, kyu, None, None, state, u_new, v_new, None)
    close_face(cx, cy, u, rate, ha, ka, u_new, v_new, send)
    pack_rows(cx, cy, u_new, ya_send, yb_send)


def finish_a(cx, cy, u, rate, ha, ka, ya, yb, u_new, v_new, send):
    put_halos(cy, sides(cx)[0], ya, yb, send)
    close_face(cx, cy, u, rate, ha, ka, u_new, v_new, send)


def close_face(cx, cy, u, rate, ha, ka, u_new, v_new, send):
    at = layer(sides(cx)[0], cy)
    fix_face(at, u, rate, ka[...], lambda c: ha[c * cy : (c + 1) * cy, :], u_new, v_new, put_face(cy, send))


def hand_on(*refs):
    del refs


def after(array, other):
    return call(hand_on, [array.shape], (array, other), {0: 0})[0]


def last_outer(
    cx, cy, u1, v1, u, rate, ha, ka, ya, yb, kyd, kyu, u_in, v_in, u_new, v_new, u_hbm, v_hbm, sems
):
    fa = sides(cx)[0]
    row = lax.broadcasted_iota(jnp.int32, (TILE, u.shape[-1]), 0)
    copies = []

    def send(layers, rows):
        for source, target in ((u_new, u_hbm), (v_new, v_hbm)):
            source, target = (ref.reshape(3, cx, cy, ref.shape[-1]).at[:, layers, rows, :] for ref in (source, target))
            copy = pltpu.make_async_copy(source, target, sems.at[len(copies)])
            copy.start()
            copies.append(copy)

    fix_face(layer(fa, cy), u, rate, ka[...], lambda c: ha[c * cy : (c + 1) * cy, :], u_new, v_new)
    send(pl.ds(fa, 1), pl.ds(TILE, cy - 2 * TILE))
    for side, (edge, stiff) in enumerate(((0, kyd), (TILE - 1, kyu))):
        offset = 0 if side == 0 else cy - TILE
        for x in range(cx):
            at = slice(x * cy + offset, x * cy + offset + TILE)
            k = jnp.where(row == edge, stiff[at, :], 0.0)
            r = rate[at, :]
            for c in range(3):
                push = r * (k * (halo_rows(ya, yb, c, x)[side] - u[c, at, :]))
                v_new[c, at, :] += push
                u_new[c, at, :] += r * push
        send(pl.ds(0, cx), pl.ds(offset, TILE))
    for copy in copies:
        copy.wait()


def per_device(displacement, velocity, body_load, damaged, eroded, material, stiff_table):
    _, cx, cy, nz = displacement.shape
    rows = cx * cy
    slabs, planes = lax.axis_size("slab"), lax.axis_size("plane")
    xa = swap_pairs(slabs, planes, True, False)
    xb = swap_pairs(slabs, planes, True, True)
    pa = swap_pairs(slabs, planes, False, False)
    pb = swap_pairs(slabs, planes, False, True)

    field, face, side, cells = (3, rows, nz), (3, cy, nz), (3, cx, nz), (rows, nz)
    u = displacement.reshape(field)
    v = velocity.reshape(field)
    load = body_load.reshape(field)
    damaged, eroded, material = (a.reshape(cells) for a in (damaged, eroded, material))

    def bind(kernel):
        return functools.partial(kernel, cx, cy)

    table_shape = (stiff_table.shape[0], nz)
    b, table, damaged = call(
        bind(open_b),
        [(4, cy, nz), table_shape, cells],
        (),
        in_hbm=(u, material, eroded, stiff_table, damaged),
        dtypes=[jnp.float32, jnp.float32, jnp.int32],
        scratch=[
            pltpu.SMEM(stiff_table.shape, jnp.float32),
            pltpu.VMEM((2, cy, nz), jnp.int32),
            pltpu.SemaphoreType.DMA((5,)),
        ],
    )
    a, ya, yb = call(
        bind(open_rest),
        [(4, cy, nz)] + [(4, cx, nz)] * 2,
        (b, u, material, eroded, table),
        scratch=[pltpu.VMEM((2, 2, cx, nz), jnp.int32)],
    )
    both = {0: 0, 1: 1}
    for sub in range(SUBSTEPS):
        last = sub == SUBSTEPS - 1
        hb = lax.ppermute(b, AXES, xb)
        if last:
            yb = after(yb, a)
        hyb = lax.ppermute(yb, AXES, pb)
        if sub == 0:
            a = after(a, yb)
        ha = lax.ppermute(a, AXES, xa)
        hya = lax.ppermute(ya, AXES, pa)
        if sub == 0:
            u_new, v_new, kx, kyd, kyu, kzd, kzu, total, coarse, fine = call(
                bind(prepare_kernel),
                [field] * 2 + [((cx + 1) * cy, nz)] + [cells] * 7,
                (u, material, eroded, table, v, load, damaged),
                scratch=[pltpu.VMEM(cells, jnp.float32)],
            )
            rate = coarse
            u_new, v, kyd, kyu, total, k_low, k_high = call(
                bind(rest_kernel_first),
                [field, field] + [cells] * 3 + [(TILE, nz)] * 2,
                (u_new, v_new, kyd, kyu, total, u, v, load, kx, kzd, kzu, rate, hya, hyb, ya, yb),
                {i: i for i in range(5)},
                scratch=[pltpu.VMEM((2, cx, nz), jnp.float32)],
            )
            u_new, v, b_next, kb = call(
                bind(fix_b_first),
                [field, field, face, (cy, nz)],
                (u_new, v, u, rate, hb, hya, hyb, b, k_low, k_high),
                both,
                weight=LONG,
            )
            sides_next = call(bind(pack_first), [(4, cx, nz)] * 2, (u_new, fine))
        elif not last:
            rate = fine
            stiff = kx, kyd, kyu, kzd, kzu, total
            u_new, v = call(bind(edge_kernel), [field, field], (u, v, load, *stiff, rate), {1: 1})
            u_new, v, b_next = call(
                bind(fix_b),
                [field, field, face],
                (u_new, v, u, rate, hb, hya, hyb, kb, k_low, k_high),
                both,
                weight=LONG,
            )
            packs = sub < SUBSTEPS - 2
            u_new, v, *sides_next = call(
                bind(rest_kernel if packs else rest_kernel_plain),
                [field, field] + ([side, side] if packs else []),
                (u_new, v, u, load, *stiff, rate, hya, hyb),
                both,
            )
        else:
            break
        b = b_next
        face_and_halos, state_shape = (3 * cy + TILE, nz), (2, 16, nz)
        if sub == 0:
            u_new, v, a, ka = call(
                bind(fix_a_first),
                [field, field, face_and_halos, (cy, nz)],
                (u_new, v, u, rate, ha, a, hya, hyb),
                both,
            )
            old = hya, hyb
        elif sub == 1:
            u_new, v, a, state = call(
                bind(fix_a_second),
                [field, field, face_and_halos, state_shape],
                (u_new, v, u, rate, ha, ka, hya, hyb, kyd, kyu, *old),
                both,
            )
        else:
            u_new, v, a, *sides_next = call(
                bind(fix_a_third),
                [field, field, (3 * cy, nz), side, side],
                (u_new, v, u, rate, ha, ka, hya, hyb, kyd, kyu, state),
                both,
            )
        u = u_new
        ya, yb = sides_next
    u_new, v, *out = call(
        bind(last_inner),
        [field, field],
        (u, v, load, *stiff, fine, hb, kb),
        {1: 1},
        scratch=[pltpu.SemaphoreType.DMA((2 * (cx - 1),))],
        to_hbm=[field, field],
    )
    out = call(
        bind(last_outer),
        [field, field],
        (u_new, v, u, fine, ha, ka, hya, hyb, kyd, kyu),
        {0: 0, 1: 1, 10: 2, 11: 3},
        in_hbm=out,
        scratch=[pltpu.SemaphoreType.DMA((6,))],
        to_hbm=[field, field],
    )
    return out[2].reshape(displacement.shape), out[3].reshape(displacement.shape)


def solution(mesh):
    field, cells = P(None, "slab", "plane", None), P("slab", "plane", None)
    return jax.shard_map(
        per_device,
        mesh=mesh,
        in_specs=(field, field, field, cells, cells, cells, P()),
        out_specs=(field, field),
        check_vma=False,
    )
```

```python
import functools

import jax
import jax.numpy as jnp
from jax import lax
from jax.experimental import pallas as pl
from jax.experimental.pallas import tpu as pltpu
from jax.sharding import PartitionSpec as P

SUBSTEPS = 4
COARSE = 0.5
FINE = COARSE / SUBSTEPS
DRAG = 0.2
TILE = 8
LONG = 1 << 30
AXES = ("slab", "plane")

VMEM = pl.BlockSpec(memory_space=pltpu.VMEM)
HBM = pl.BlockSpec(memory_space=pltpu.HBM)
SMALL = pltpu.CompilerParams(vmem_limit_bytes=2 << 20)


def partner(index, count, second):
    other = ((index - 1) ^ 1) + 1 if second else index ^ 1
    return other if 0 <= other < count and (index or not second) else None


def swap_pairs(slabs, planes, along_slab, second):
    pairs = []
    for s in range(slabs):
        for p in range(planes):
            if along_slab:
                other = partner(s, slabs, second)
                target = (other, p) if other is not None else (s, p ^ 1 if (p ^ 1) < planes else None)
            else:
                other = partner(p, planes, second)
                rest = planes - 1 - p if planes % 2 == 0 else None
                target = (s, other if other is not None else rest)
            if target[1] is not None and target != (s, p):
                pairs.append((s * planes + p, target[0] * planes + target[1]))
    return pairs


def has_partner(index, count, second):
    even = index % 2 == 0
    up = jnp.logical_not(even) if second else even
    return jnp.where(up, index + 1 < count, index > 0)


def pin(arrays, space):
    return [pltpu.with_memory_space_constraint(a, space) for a in arrays]


def call(kernel, shapes, arrays, aliases=None, in_hbm=(), dtypes=None, scratch=(), to_hbm=(), weight=1):
    dtypes = dtypes or [jnp.float32] * len(shapes)
    out_shape = [pltpu.VMEM(s, t) for s, t in zip(shapes, dtypes)]
    out_shape += [pltpu.HBM(s, jnp.float32) for s in to_hbm]
    return pl.pallas_call(
        kernel,
        in_specs=[VMEM] * len(arrays) + [HBM] * len(in_hbm),
        out_specs=[VMEM] * len(shapes) + [HBM] * len(to_hbm),
        out_shape=out_shape,
        scratch_shapes=scratch,
        input_output_aliases=aliases or {},
        compiler_params=SMALL,
        cost_estimate=pl.CostEstimate(flops=weight, bytes_accessed=weight, transcendentals=0),
    )(*pin(arrays, pltpu.VMEM), *pin(in_hbm, pltpu.HBM))


def lookup(material, eroded, table):
    total = jnp.zeros(material.shape, jnp.float32)
    for index in range(table.shape[0]):
        total = jnp.where(material == index, table[index : index + 1, :], total)
    return total * (1 - eroded).astype(jnp.float32)


def run(start, rows, step=TILE):
    return pl.ds(start if isinstance(start, int) else pl.multiple_of(start, step), rows)


def layer(index, rows):
    return run(index * rows, rows, rows)


def sides(cx):
    slab = lax.axis_index("slab")
    even = slab % 2 == 0
    return jnp.where(even, cx - 1, 0), jnp.where(even, 0, cx - 1)


def plane_even():
    return lax.axis_index("plane") % 2 == 0


def start_copies(moves, sems):
    copies = [pltpu.make_async_copy(source, target, sems.at[i]) for i, (source, target) in enumerate(moves)]
    for copy in copies:
        copy.start()
    return copies


def open_b(
    cx, cy, u_hbm, material_hbm, eroded_hbm, table_hbm, damaged_hbm, b, table, damaged, scalars, cells, sems
):
    at = layer(sides(cx)[1], cy)
    moves = [(table_hbm, scalars), (material_hbm.at[at, :], cells.at[0]), (eroded_hbm.at[at, :], cells.at[1])]
    moves += [(u_hbm.at[:, at, :], b.at[pl.ds(0, 3)]), (damaged_hbm, damaged)]
    copies = start_copies(moves, sems)
    copies[0].wait()
    for index in range(table.shape[0]):
        table[index : index + 1, :] = jnp.full((1, table.shape[1]), scalars[index], jnp.float32)
    copies[1].wait()
    copies[2].wait()
    b[3] = lookup(cells[0], cells[1], table)
    copies[3].wait()
    copies[4].wait()


def open_rest(cx, cy, b_sent, u, material, eroded, table, a, ya, yb, edge):
    even = plane_even()
    at = layer(sides(cx)[0], cy)
    a[3] = lookup(material[at, :], eroded[at, :], table)
    for c in range(3):
        a[c] = u[c, at, :]
    for x in range(cx):
        top, end = slice(x * cy, x * cy + TILE), slice((x + 1) * cy - TILE, (x + 1) * cy)
        for i, cells in enumerate((material, eroded)):
            put_rows(even, x, i, cells[top, :], cells[end, :], edge.at[0], edge.at[1])
    for side, out in enumerate((ya, yb)):
        out[3] = lookup(edge[side, 0], edge[side, 1], table)
    pack_rows(cx, cy, u, ya, yb)


def put_rows(even, x, c, first, last, ya, yb):
    first, last = first[0:1, :], last[TILE - 1 : TILE, :]
    ya[c, x : x + 1, :] = jnp.where(even, last, first)
    yb[c, x : x + 1, :] = jnp.where(even, first, last)


def advance(cx, cy, first, count, u, v, load, stiff, rate, u_out, v_out, halo=None, then=None, tiles=None):
    kx, ky_down, ky_up, kz_down, kz_up, total = stiff
    nz = u.shape[-1]
    row = lax.broadcasted_iota(jnp.int32, (TILE, nz), 0)
    even = plane_even()

    def tile(x, t):
        return run(x * cy + t * TILE, TILE)

    def clamp(x):
        return min(max(x, 0), cx - 1) if isinstance(x, int) else jnp.clip(x, 0, cx - 1)

    for i in range(count):
        x = first + i
        for t in tiles if tiles is not None else range(cy // TILE):
            at = tile(x, t)
            x_down, x_up = tile(clamp(x - 1), t), tile(clamp(x + 1), t)
            r = rate[at, :]
            for c in range(3):
                here = u[c, at, :]
                one, two = (h[c, pl.ds(x, 1), :] for h in halo) if halo else (here, here)
                if t > 0:
                    down = pltpu.roll(u[c, tile(x, t - 1), :], 1, 0)
                else:
                    down = jnp.where(even, two, one)
                if t < cy // TILE - 1:
                    up = pltpu.roll(u[c, tile(x, t + 1), :], TILE - 1, 0)
                else:
                    up = jnp.where(even, one, two)
                down = jnp.where(row == 0, down, pltpu.roll(here, 1, 0))
                up = jnp.where(row == TILE - 1, up, pltpu.roll(here, TILE - 1, 0))
                force = (kx[at, :] * u[c, x_down, :] + kx[tile(x + 1, t), :] * u[c, x_up, :]) - total[at, :] * here
                force = force + (ky_down[at, :] * down + ky_up[at, :] * up)
                force = force + (
                    kz_down[at, :] * pltpu.roll(here, 1, 1) + kz_up[at, :] * pltpu.roll(here, nz - 1, 1)
                )
                speed = v[c, at, :]
                speed = speed + r * (force + load[c, at, :] - DRAG * speed)
                v_out[c, at, :] = speed
                u_out[c, at, :] = here + r * speed
        if then is not None:
            then(i)


def rest_first(cx):
    return jnp.where(sides(cx)[1] == 0, 1, 0)


def advance_inner(cx, cy, u, v, load, stiff, rate, u_out, v_out):
    advance(cx, cy, sides(cx)[1], 1, u, v, load, stiff, rate, u_out, v_out)
    inner = range(1, cy // TILE - 1)
    advance(cx, cy, rest_first(cx), cx - 1, u, v, load, stiff, rate, u_out, v_out, tiles=inner)


def advance_outer(cx, cy, u, v, load, stiff, rate, u_out, v_out, halo, then=None):
    outer = sorted({0, cy // TILE - 1})
    advance(cx, cy, rest_first(cx), cx - 1, u, v, load, stiff, rate, u_out, v_out, halo, then, outer)


def edge_kernel(cx, cy, u, v, load, kx, kyd, kyu, kzd, kzu, total, rate, u_out, v_out):
    advance_inner(cx, cy, u, v, load, (kx, kyd, kyu, kzd, kzu, total), rate, u_out, v_out)


def rest_kernel(
    cx, cy, u1, v, u, load, kx, kyd, kyu, kzd, kzu, total, rate, ya, yb, u_out, v_out, ya_send, yb_send
):
    stiff = kx, kyd, kyu, kzd, kzu, total
    advance_outer(cx, cy, u, v, load, stiff, rate, u_out, v_out, (ya, yb))
    pack_rows(cx, cy, u_out, ya_send, yb_send)


def rest_kernel_plain(cx, cy, u1, v, u, load, kx, kyd, kyu, kzd, kzu, total, rate, ya, yb, u_out, v_out):
    stiff = kx, kyd, kyu, kzd, kzu, total
    advance_outer(cx, cy, u, v, load, stiff, rate, u_out, v_out, (ya, yb))


def last_inner(
    cx, cy, u, v, load, kx, kyd, kyu, kzd, kzu, total, rate, hb, kb, u_out, v_out, u_hbm, v_hbm, sems
):
    stiff = kx, kyd, kyu, kzd, kzu, total
    fa, fb = sides(cx)
    copies = []

    def send(x):
        at = run(x * cy + TILE, cy - 2 * TILE)
        for source, target in ((u_out, u_hbm), (v_out, v_hbm)):
            copy = pltpu.make_async_copy(source.at[:, at, :], target.at[:, at, :], sems.at[len(copies)])
            copy.start()
            copies.append(copy)

    advance(cx, cy, fb, 1, u, v, load, stiff, rate, u_out, v_out)
    fix_face(layer(fb, cy), u, rate, kb[...], lambda c: hb[c], u_out, v_out)
    send(fb)
    advance(cx, cy, 1, cx - 2, u, v, load, stiff, rate, u_out, v_out, then=lambda i: send(1 + i))
    advance(cx, cy, fa, 1, u, v, load, stiff, rate, u_out, v_out)
    for copy in copies:
        copy.wait()


def rest_kernel_first(
    cx, cy, u1, v1, kyd, kyu, total, u, v, load, kx, kzd, kzu, rate, ya, yb, ya_sent, yb_sent,
    u_out, v_out, kyd_out, kyu_out, total_out, k_low, k_high, sides_k,
):
    low, high = row_stiffness(ya_sent, yb_sent, ya, yb)
    sides_k[0], sides_k[1] = low, high
    row = lax.broadcasted_iota(jnp.int32, (TILE, u.shape[-1]), 0)
    face = sides(cx)[1]
    k_low[...] = jnp.where(row == 0, sides_k[0, pl.ds(face, 1), :], 0.0)
    k_high[...] = jnp.where(row == TILE - 1, sides_k[1, pl.ds(face, 1), :], 0.0)
    for x in range(cx):
        for start, edge, k, out in (
            (x * cy, 0, low, kyd_out),
            ((x + 1) * cy - TILE, TILE - 1, high, kyu_out),
        ):
            at = slice(start, start + TILE)
            extra = jnp.where(row == edge, k[x : x + 1, :], 0.0)
            out[at, :] += extra
            total_out[at, :] += extra
    stiff = kx, kyd_out, kyu_out, kzd, kzu, total_out
    advance_outer(cx, cy, u, v, load, stiff, rate, u_out, v_out, (ya, yb))


def pack_first(cx, cy, u_new, fine, ya_send, yb_send):
    pack_rows(cx, cy, u_new, ya_send, yb_send, fine)


def prepare_kernel(
    cx, cy, u, material, eroded, table, v, load, damaged,
    u_out, v_out, kx, kyd, kyu, kzd, kzu, total, coarse, fine, k_all,
):
    nz = u.shape[-1]
    row = lax.broadcasted_iota(jnp.int32, (TILE, nz), 0)
    lane = lax.broadcasted_iota(jnp.int32, (TILE, nz), 1)
    nothing = jnp.zeros((TILE, nz), jnp.float32)
    tiles = cy // TILE
    for start in range(0, cx * cy, TILE):
        at = slice(start, start + TILE)
        k_all[at, :] = lookup(material[at, :], eroded[at, :], table)
    for t in range(tiles):
        face = nothing
        for x in range(cx):
            start = x * cy + t * TILE
            at = slice(start, start + TILE)
            k = k_all[at, :]
            y_up = k_all[start + TILE : start + TILE + 1, :] if t < tiles - 1 else 0.0
            y_down = k_all[start - 1 : start, :] if t > 0 else 0.0
            y_up = jnp.minimum(k, jnp.where(row == TILE - 1, y_up, pltpu.roll(k, TILE - 1, 0)))
            y_down = jnp.minimum(k, jnp.where(row == 0, y_down, pltpu.roll(k, 1, 0)))
            z_up = jnp.minimum(k, jnp.where(lane == nz - 1, 0.0, pltpu.roll(k, nz - 1, 1)))
            z_down = jnp.minimum(k, jnp.where(lane == 0, 0.0, pltpu.roll(k, 1, 1)))
            face_up = jnp.minimum(k, k_all[start + cy : start + cy + TILE, :]) if x < cx - 1 else nothing
            for out, value in ((kx, face), (kyu, y_up), (kyd, y_down), (kzu, z_up), (kzd, z_down)):
                out[at, :] = value
            total[at, :] = ((face + face_up) + (y_up + y_down)) + (z_up + z_down)
            face = face_up
    kx[cx * cy : (cx + 1) * cy, :] = jnp.zeros((cy, nz), jnp.float32)
    for x in range(cx):
        at = slice(x * cy, (x + 1) * cy)
        hit = damaged[at, :] == 1
        coarse[at, :] = jnp.where(hit, FINE, COARSE)
        fine[at, :] = jnp.where(hit, FINE, 0.0)
    stiff = kx, kyd, kyu, kzd, kzu, total
    advance_inner(cx, cy, u, v, load, stiff, coarse, u_out, v_out)


def fix_face(at, u, rate, k, halo, u_new, v_new, put=None):
    r = rate[at, :]
    for c in range(3):
        push = r * (k * (halo(c) - u[c, at, :]))
        v_new[c, at, :] += push
        moved = u_new[c, at, :] + r * push
        u_new[c, at, :] = moved
        if put is not None:
            put(c, moved)


def fix_rows(cy, x, u, rate, k_low, k_high, ya, yb, u_new, v_new):
    even = plane_even()
    for start, k, flip in ((x * cy, k_low, False), ((x + 1) * cy - TILE, k_high, True)):
        at = pl.ds(pl.multiple_of(start, TILE), TILE)
        r = rate[at, :]
        for c in range(3):
            one, two = ya[c, pl.ds(x, 1), :], yb[c, pl.ds(x, 1), :]
            halo = jnp.where(even, one, two) if flip else jnp.where(even, two, one)
            push = r * (k[...] * (halo - u[c, at, :]))
            v_new[c, at, :] += push
            u_new[c, at, :] += r * push


def pack_rows(cx, cy, u_new, ya_send, yb_send, cells=None):
    even = plane_even()
    for c in range(3 if cells is None else 4):
        for x in range(cx):
            top, end = slice(x * cy, x * cy + TILE), slice((x + 1) * cy - TILE, (x + 1) * cy)
            if c < 3:
                first, last = u_new[c, top, :], u_new[c, end, :]
            else:
                first, last = cells[top, :], cells[end, :]
            put_rows(even, x, c, first, last, ya_send, yb_send)


def flag(axis, second):
    return has_partner(lax.axis_index(axis), lax.axis_size(axis), second).astype(jnp.float32)


def face_stiffness(sent, received, second):
    return jnp.minimum(sent[3], received[3]) * flag("slab", second)


def row_stiffness(ya_sent, yb_sent, ya, yb):
    even = plane_even()
    k_a = jnp.minimum(ya_sent[3], ya[3]) * flag("plane", False)
    k_b = jnp.minimum(yb_sent[3], yb[3]) * flag("plane", True)
    return jnp.where(even, k_b, k_a), jnp.where(even, k_a, k_b)


def fix_b_first(cx, cy, u1, v1, u, rate, hb, ya, yb, b_sent, k_low, k_high, u_new, v_new, send, kb):
    kb[...] = face_stiffness(b_sent, hb, True)
    fix_b(cx, cy, u1, v1, u, rate, hb, ya, yb, kb, k_low, k_high, u_new, v_new, send)


def fix_b(cx, cy, u1, v1, u, rate, hb, ya, yb, kb, k_low, k_high, u_new, v_new, send=None):
    face = sides(cx)[1]
    fix_rows(cy, face, u, rate, k_low, k_high, ya, yb, u_new, v_new)

    def put(c, moved):
        if send is not None:
            send[c] = moved

    fix_face(layer(face, cy), u, rate, kb[...], lambda c: hb[c], u_new, v_new, put)


def put_face(cy, send):
    def put(c, moved):
        send[c * cy : (c + 1) * cy, :] = moved

    return put


def put_halos(cy, x, ya, yb, send):
    for c in range(4):
        if c < ya.shape[0]:
            rows = halo_rows(ya, yb, c, x)
        else:
            rows = [jnp.zeros((1, send.shape[1]), jnp.float32)] * 2
        for side in range(2):
            at = 3 * cy + 4 * side + c
            send[at : at + 1, :] = rows[side]


def halo_rows(ya, yb, c, x):
    even = plane_even()
    one, two = ya[c, pl.ds(x, 1), :], yb[c, pl.ds(x, 1), :]
    return jnp.where(even, two, one), jnp.where(even, one, two)


def coarse_of(fine):
    return COARSE + (FINE - COARSE) / FINE * fine


def correct(cx, cy, step, rate, ha, ya, yb, kyd, kyu, old_ya, old_yb, state, u_new, v_new, state_out):
    face = sides(cx)[0]
    row = lax.broadcasted_iota(jnp.int32, (TILE, rate.shape[1]), 0)
    for side in range(2):
        def sent(f, base=3 * cy + 4 * side):
            return ha[base + f : base + f + 1, :]

        def kept(f, side=side):
            return state[side, f : f + 1, :]

        if step == 1:
            k = jnp.minimum(halo_rows(old_ya, old_yb, 3, face)[side], sent(3)) * flag("slab", False)
            mine = halo_rows(ya, yb, 3, face)[side]
            other = jnp.zeros_like(mine)
            scale = coarse_of(mine) * coarse_of(mine) * k
        else:
            k, mine = kept(9), kept(10)
            other = sent(3) if step == 2 else kept(11)
            scale = mine * mine * k
            pace = coarse_of(other) if step == 2 else other
            pace = pace * pace * k
        start = face * cy if side == 0 else (face + 1) * cy - TILE
        at = pl.ds(pl.multiple_of(start, TILE), TILE)
        edge_k = jnp.where(row == (0 if side == 0 else TILE - 1), (kyd if side == 0 else kyu)[at, :], 0.0)
        r = rate[at, :]
        for c in range(3):
            if step == 1:
                before, across = halo_rows(old_ya, old_yb, c, face)[side], sent(c)
            else:
                before = kept(c)
                across = sent(c) + pace * (kept(3 + c) - kept(6 + c))
            late = scale * (across - before)
            push = r * (edge_k * late)
            v_new[c, at, :] += push
            u_new[c, at, :] += r * push
            if state_out is not None:
                now = halo_rows(ya, yb, c, face)[side] + late
                for f, value in ((c, now), (3 + c, before), (6 + c, across)):
                    state_out[side, f : f + 1, :] = value
        if state_out is not None:
            for f, value in ((9, k), (10, mine), (11, other)):
                state_out[side, f : f + 1, :] = value


def fix_a_first(cx, cy, u1, v1, u, rate, ha, a_sent, ya, yb, u_new, v_new, send, ka):
    ka[...] = face_stiffness(a_sent, ha, False)
    face = sides(cx)[0]
    put_halos(cy, face, ya, yb, send)
    fix_face(layer(face, cy), u, rate, ka[...], lambda c: ha[c], u_new, v_new, put_face(cy, send))


def fix_a_second(
    cx, cy, u1, v1, u, rate, ha, ka, ya, yb, kyd, kyu, old_ya, old_yb, u_new, v_new, send, state_out
):
    correct(cx, cy, 1, rate, ha, ya, yb, kyd, kyu, old_ya, old_yb, None, u_new, v_new, state_out)
    finish_a(cx, cy, u, rate, ha, ka, ya, yb, u_new, v_new, send)


def fix_a_third(
    cx, cy, u1, v1, u, rate, ha, ka, ya, yb, kyd, kyu, state, u_new, v_new, send, ya_send, yb_send
):
    correct(cx, cy, 2, rate, ha, ya, yb, kyd, kyu, None, None, state, u_new, v_new, None)
    close_face(cx, cy, u, rate, ha, ka, u_new, v_new, send)
    pack_rows(cx, cy, u_new, ya_send, yb_send)


def finish_a(cx, cy, u, rate, ha, ka, ya, yb, u_new, v_new, send):
    put_halos(cy, sides(cx)[0], ya, yb, send)
    close_face(cx, cy, u, rate, ha, ka, u_new, v_new, send)


def close_face(cx, cy, u, rate, ha, ka, u_new, v_new, send):
    at = layer(sides(cx)[0], cy)
    fix_face(at, u, rate, ka[...], lambda c: ha[c * cy : (c + 1) * cy, :], u_new, v_new, put_face(cy, send))


def hand_on(*refs):
    del refs


def after(array, other):
    return call(hand_on, [array.shape], (array, other), {0: 0})[0]


def last_outer(
    cx, cy, u1, v1, u, rate, ha, ka, yb, kyd, kyu, u_in, v_in, u_new, v_new, u_hbm, v_hbm, sems
):
    fa = sides(cx)[0]
    copies = []

    def send(layers, rows):
        for source, target in ((u_new, u_hbm), (v_new, v_hbm)):
            source, target = (ref.reshape(3, cx, cy, ref.shape[-1]).at[:, layers, rows, :] for ref in (source, target))
            copy = pltpu.make_async_copy(source, target, sems.at[len(copies)])
            copy.start()
            copies.append(copy)

    fix_face(layer(fa, cy), u, rate, ka[...], lambda c: ha[c * cy : (c + 1) * cy, :], u_new, v_new)
    even = plane_even()
    ready = jnp.where(even, cy - TILE, 0)
    send(pl.ds(0, cx), run(ready, TILE))
    send(pl.ds(fa, 1), pl.ds(TILE, cy - 2 * TILE))
    for x in range(cx):
        fix_edge(cx, cy, x, True, u, rate, yb, kyd, kyu, u_new, v_new)
    send(pl.ds(0, cx), run(cy - TILE - ready, TILE))
    for copy in copies:
        copy.wait()


def last_first_plane(cx, cy, u1, v1, u, rate, ya, kyd, kyu, u_new, v_new):
    for x in range(cx):
        fix_edge(cx, cy, x, False, u, rate, ya, kyd, kyu, u_new, v_new)


def fix_edge(cx, cy, x, second, u, rate, halo, kyd, kyu, u_new, v_new):
    even = plane_even()
    high = jnp.logical_not(even) if second else even
    at = run(jnp.where(high, (x + 1) * cy - TILE, x * cy), TILE)
    row = lax.broadcasted_iota(jnp.int32, (TILE, u.shape[-1]), 0)
    edge = jnp.where(high, TILE - 1, 0)
    k = jnp.where(row == edge, jnp.where(high, kyu[at, :], kyd[at, :]), 0.0)
    r = rate[at, :]
    for c in range(3):
        push = r * (k * (halo[c, x : x + 1, :] - u[c, at, :]))
        v_new[c, at, :] += push
        u_new[c, at, :] += r * push


def per_device(displacement, velocity, body_load, damaged, eroded, material, stiff_table):
    _, cx, cy, nz = displacement.shape
    rows = cx * cy
    slabs, planes = lax.axis_size("slab"), lax.axis_size("plane")
    xa = swap_pairs(slabs, planes, True, False)
    xb = swap_pairs(slabs, planes, True, True)
    pa = swap_pairs(slabs, planes, False, False)
    pb = swap_pairs(slabs, planes, False, True)

    field, face, side, cells = (3, rows, nz), (3, cy, nz), (3, cx, nz), (rows, nz)
    u = displacement.reshape(field)
    v = velocity.reshape(field)
    load = body_load.reshape(field)
    damaged, eroded, material = (a.reshape(cells) for a in (damaged, eroded, material))

    def bind(kernel):
        return functools.partial(kernel, cx, cy)

    table_shape = (stiff_table.shape[0], nz)
    b, table, damaged = call(
        bind(open_b),
        [(4, cy, nz), table_shape, cells],
        (),
        in_hbm=(u, material, eroded, stiff_table, damaged),
        dtypes=[jnp.float32, jnp.float32, jnp.int32],
        scratch=[
            pltpu.SMEM(stiff_table.shape, jnp.float32),
            pltpu.VMEM((2, cy, nz), jnp.int32),
            pltpu.SemaphoreType.DMA((5,)),
        ],
    )
    a, ya, yb = call(
        bind(open_rest),
        [(4, cy, nz)] + [(4, cx, nz)] * 2,
        (b, u, material, eroded, table),
        scratch=[pltpu.VMEM((2, 2, cx, nz), jnp.int32)],
    )
    both = {0: 0, 1: 1}
    for sub in range(SUBSTEPS):
        last = sub == SUBSTEPS - 1
        hb = lax.ppermute(b, AXES, xb)
        if last:
            yb = after(yb, a)
        hyb = lax.ppermute(yb, AXES, pb)
        if sub == 0:
            a = after(a, yb)
        ha = lax.ppermute(a, AXES, xa)
        hya = lax.ppermute(ya, AXES, pa)
        if sub == 0:
            u_new, v_new, kx, kyd, kyu, kzd, kzu, total, coarse, fine = call(
                bind(prepare_kernel),
                [field] * 2 + [((cx + 1) * cy, nz)] + [cells] * 7,
                (u, material, eroded, table, v, load, damaged),
                scratch=[pltpu.VMEM(cells, jnp.float32)],
            )
            rate = coarse
            u_new, v, kyd, kyu, total, k_low, k_high = call(
                bind(rest_kernel_first),
                [field, field] + [cells] * 3 + [(TILE, nz)] * 2,
                (u_new, v_new, kyd, kyu, total, u, v, load, kx, kzd, kzu, rate, hya, hyb, ya, yb),
                {i: i for i in range(5)},
                scratch=[pltpu.VMEM((2, cx, nz), jnp.float32)],
            )
            u_new, v, b_next, kb = call(
                bind(fix_b_first),
                [field, field, face, (cy, nz)],
                (u_new, v, u, rate, hb, hya, hyb, b, k_low, k_high),
                both,
                weight=LONG,
            )
            sides_next = call(bind(pack_first), [(4, cx, nz)] * 2, (u_new, fine))
        elif not last:
            rate = fine
            stiff = kx, kyd, kyu, kzd, kzu, total
            u_new, v = call(bind(edge_kernel), [field, field], (u, v, load, *stiff, rate), {1: 1})
            u_new, v, b_next = call(
                bind(fix_b),
                [field, field, face],
                (u_new, v, u, rate, hb, hya, hyb, kb, k_low, k_high),
                both,
                weight=LONG,
            )
            packs = sub < SUBSTEPS - 2
            u_new, v, *sides_next = call(
                bind(rest_kernel if packs else rest_kernel_plain),
                [field, field] + ([side, side] if packs else []),
                (u_new, v, u, load, *stiff, rate, hya, hyb),
                both,
            )
        else:
            break
        b = b_next
        face_and_halos, state_shape = (3 * cy + TILE, nz), (2, 16, nz)
        if sub == 0:
            u_new, v, a, ka = call(
                bind(fix_a_first),
                [field, field, face_and_halos, (cy, nz)],
                (u_new, v, u, rate, ha, a, hya, hyb),
                both,
            )
            old = hya, hyb
        elif sub == 1:
            u_new, v, a, state = call(
                bind(fix_a_second),
                [field, field, face_and_halos, state_shape],
                (u_new, v, u, rate, ha, ka, hya, hyb, kyd, kyu, *old),
                both,
            )
        else:
            u_new, v, a, *sides_next = call(
                bind(fix_a_third),
                [field, field, (3 * cy, nz), side, side],
                (u_new, v, u, rate, ha, ka, hya, hyb, kyd, kyu, state),
                both,
            )
        u = u_new
        ya, yb = sides_next
    u_new, v, *out = call(
        bind(last_inner),
        [field, field],
        (u, v, load, *stiff, fine, hb, kb),
        {1: 1},
        scratch=[pltpu.SemaphoreType.DMA((2 * (cx - 1),))],
        to_hbm=[field, field],
    )
    u_new, v = call(bind(last_first_plane), [field, field], (u_new, v, u, fine, hya, kyd, kyu), both)
    out = call(
        bind(last_outer),
        [field, field],
        (u_new, v, u, fine, ha, ka, hyb, kyd, kyu),
        {0: 0, 1: 1, 9: 2, 10: 3},
        in_hbm=out,
        scratch=[pltpu.SemaphoreType.DMA((6,))],
        to_hbm=[field, field],
    )
    return out[2].reshape(displacement.shape), out[3].reshape(displacement.shape)


def solution(mesh):
    field, cells = P(None, "slab", "plane", None), P("slab", "plane", None)
    return jax.shard_map(
        per_device,
        mesh=mesh,
        in_specs=(field, field, field, cells, cells, cells, P()),
        out_specs=(field, field),
        check_vma=False,
    )
```
